256 devices in a mesh: ctx: 8 (over y, x_hi), dp: 16 (over x_lo, z), tp: 2 (over core).
Axes of the slice: x: 4 (x_hi: 2, x_lo: 2; x = x_hi * 2 + x_lo), y: 4, z: 8, core: 2. Of those that a mesh axis runs over, the one named last changes fastest.
Arguments:
- layer_input: bfloat16 [16, 2048, 8192], P('dp', 'ctx', 'tp'), may hold values from -6 to 6
- queries: bfloat16 [16, 2048, 4096], P('dp', 'ctx', 'tp'), may hold values from -64 to 64
- keys: bfloat16 [16, 2048, 512], P('dp', 'ctx', 'tp'), may hold values from -8 to 8
- values: bfloat16 [16, 2048, 512], P('dp', 'ctx', 'tp'), may hold values from -6 to 6
- out_grad: bfloat16 [16, 2048, 4096], P('dp', 'ctx', 'tp'), may hold values from -6 to 6
- doc_ids: int32 [16, 2048], P('dp', 'ctx'), may hold values from 0 to 3, never falling along the last dimension, each value on 1 to 1024 neighbouring positions
- freq_bins: int32 [64], replicated, may hold values from 0 to 32
- master: float32 [2, 4096, 512], P(None, 'dp', 'tp'), may hold values from -0.0625 to 0.0625
- moment1: float32 [2, 4096, 512], P(None, 'dp', 'tp'), may hold values from -3 to 3
- moment2: float32 [2, 4096, 512], P(None, 'dp', 'tp'), may hold values from 0.002 to 0.2
Outputs:
- query_grad: bfloat16 [16, 2048, 4096], P('dp', 'ctx', 'tp')
- value_grad: bfloat16 [16, 2048, 512], P('dp', 'ctx', 'tp')
- new_master: float32 [2, 4096, 512], P(None, 'dp', 'tp')
- new_moment1: float32 [2, 4096, 512], P(None, 'dp', 'tp')
- new_moment2: float32 [2, 4096, 512], P(None, 'dp', 'tp')
- key_weight: bfloat16 [2, 4096, 512], P(None, None, 'tp')
The draws below stay inside these ranges and needn't reach their ends.
Inputs may be any that keep to these rules, and one draw needn't show every extreme that they name: `doc_ids`: each sequence holds 4 documents one after another, ids never falling along the sequence.
All inputs are finite; a program needn't handle non-finite values.
Results may differ from the reference program's by a relative error of at most 0.0079.
Values may be sent and summed in bfloat16 or wider, within the bound.
A program may use at most 128 MiB of HBM per device.

```python
import math
import jax
import jax.numpy as jnp
import numpy as np
from jax import lax

D = 8192
HQ = 32
HK = 4
HD = 128
BINS = 32
DOCS = 4
ADAM_STEP = 10
SEQS = 16
LEN = 2048
ROW_GROUPS = 2


def paired_draw(key):
    base = jax.random.fold_in(key, 7)
    key_query, key_key = jax.random.split(base, 2)
    query_shape = (SEQS, LEN, HQ, HD)
    key_shape = (SEQS, LEN, HK, HD)
    query_out = jax.random.truncated_normal(key_query, -6.0, 6.0, query_shape, jnp.float32)
    key_out = jax.random.truncated_normal(key_key, -6.0, 6.0, key_shape, jnp.float32)
    return (query_out.reshape(SEQS, LEN, HQ * HD).astype(jnp.bfloat16), key_out.reshape(SEQS, LEN, HK * HD).astype(jnp.bfloat16))


def draw_queries(key, part):
    return paired_draw(key)[0]


def draw_keys(key, part):
    return paired_draw(key)[1]


def plant(result, rng, least, largest):
    index_at = [jax.random.randint(jax.random.fold_in(rng, axis), (), 0, length) for axis, length in enumerate(result.shape)]
    longest = result.shape.index(max(result.shape))
    beside = index_at[:longest] + [(index_at[longest] + 1) % result.shape[longest]] + index_at[longest + 1:]
    return result.at[tuple(index_at)].set(least).at[tuple(beside)].set(largest)


def raised(array, key, source, target, parts, factor):
    def block_of(position):
        return (jnp.arange(array.shape[position]) // (array.shape[position] // parts)).reshape((-1,) + (1,) * (array.ndim - 1 - position))

    first = jax.random.permutation(key, parts)[block_of(target)]
    far = (block_of(target) + parts // 2) % parts
    return jnp.where((block_of(source) == first) | (block_of(source) == far), factor * array, array)


def steps_of(rng, shape, cuts, least, largest):
    loudness = 1.0
    for axis_at, shards_of in cuts:
        steps = jax.random.uniform(jax.random.fold_in(jax.random.fold_in(rng, 6), axis_at), (shards_of,), jnp.float32, least / len(cuts), largest / len(cuts))
        loudness = loudness * jnp.repeat(jnp.exp(steps), shape[axis_at] // shards_of).reshape((-1,) + (1,) * (len(shape) - 1 - axis_at))
    return loudness


def split_up(amount, total, bound, slope):
    portions = [(1 << 20) // math.isqrt(standing ** slope) + 1 for standing in range(2, amount + 1)]
    rest, counts = total - bound - (amount - 1), [1] * (amount - 1)
    while rest > 0:
        candidates = [i for i in range(amount - 1) if counts[i] < bound]
        pool, budget = sum([portions[i] for i in candidates]), rest
        for i in candidates:
            more = min(bound - counts[i], max(1, budget * portions[i] // pool), rest)
            counts[i] = counts[i] + more
            rest = rest - more
    return np.array([bound] + counts)


def uneven_parts(key, number_of, total, limit, skew):
    if number_of == 2:
        one = jax.random.randint(key, (), max(1, total - limit), min(limit, total - 1) + 1)
        return jnp.stack([one, total - one])
    lengths = jnp.asarray(split_up(number_of, total, limit, skew), jnp.int32)
    couples = (number_of - 1) // 2
    source_of, sink = lengths[1:1 + 2 * couples:2], lengths[2:2 + 2 * couples:2]
    slack = jnp.minimum(source_of - 1, limit - sink)
    shifted = jax.random.randint(jax.random.fold_in(key, 1), (couples,), 0, 1 << 20) % (slack + 1)
    lengths = lengths.at[1:1 + 2 * couples:2].set(source_of - shifted).at[2:2 + 2 * couples:2].set(sink + shifted)
    return lengths[jax.random.permutation(jax.random.fold_in(key, 2), number_of)]


def normal_values(rng, shape, width, limit, cuts=(), dtype=jnp.bfloat16):
    entries = jax.random.normal(rng, shape, jnp.float32) * width
    if len(cuts) > 0:
        entries = steps_of(rng, shape, cuts, -0.22, 0.18) * entries
    return jnp.clip(entries, min=-limit, max=limit).astype(dtype)


def heavy_noise(stream_key, dims, spread, reach, cuts, heavy, dtype=jnp.bfloat16):
    entries = spread * jax.random.normal(stream_key, dims, jnp.float32)
    if cuts:
        entries = entries * steps_of(stream_key, dims, cuts, -0.22, 0.18)
    return jnp.clip(raised(entries, jax.random.fold_in(stream_key, 3), *heavy), -reach, reach).astype(dtype)


def setup_inputs(seed: int = 0) -> dict:
    arg_keys = jax.random.split(jax.random.key(seed), 11)
    layer_input = heavy_noise(arg_keys[0], (SEQS, LEN, D), 1.0, 6.0, ((0, 16), (1, 8), (2, 2)), (0, 2, 16, 2.0))
    queries = draw_queries(jax.random.fold_in(arg_keys[10], 71), 0)
    keys = draw_keys(jax.random.fold_in(arg_keys[10], 71), 0)
    values = normal_values(arg_keys[3], (SEQS, LEN, HK * HD), 1.0, 6.0, ((0, 16), (1, 8), (2, 2)))
    out_grad = normal_values(arg_keys[4], (SEQS, LEN, HQ * HD), 1.0, 6.0, ((0, 16), (1, 8), (2, 2)))
    doc_ids = jax.vmap(lambda own: jnp.searchsorted(jnp.cumsum(uneven_parts(own, DOCS, LEN, LEN // 2, 0)), jnp.arange(LEN), side="right"))(jax.random.split(arg_keys[5], SEQS)).reshape((SEQS, LEN)).astype(jnp.int32)
    freq_bins = plant(jax.random.randint(arg_keys[6], (HD // 2,), 0, BINS + 1), jax.random.fold_in(arg_keys[6], 1), 0, BINS).astype(jnp.int32)
    master = normal_values(arg_keys[7], (ROW_GROUPS, D // ROW_GROUPS, HK * HD), D ** -0.5, 0.0625, ((1, 16), (2, 2)), jnp.float32)
    moment1 = normal_values(arg_keys[8], (ROW_GROUPS, D // ROW_GROUPS, HK * HD), 0.2, 3.0, ((1, 16), (2, 2)), jnp.float32)
    moment2 = jnp.clip(jnp.exp(math.log(0.2) - 4.6051702 * jax.random.uniform(arg_keys[9], (ROW_GROUPS, D // ROW_GROUPS, HK * HD), jnp.float32) ** steps_of(arg_keys[9], (ROW_GROUPS, D // ROW_GROUPS, HK * HD), ((1, 16), (2, 2)), -0.2, 0.2)), 0.002, 0.2)
    return {"layer_input": layer_input, "queries": queries, "keys": keys, "values": values, "out_grad": out_grad, "doc_ids": doc_ids, "freq_bins": freq_bins, "master": master, "moment1": moment1, "moment2": moment2}


rope_base = 10000.0
yarn_factor = 8.0
magnitude_scale = 0.1 * math.log(8.0) + 1.0
beta_first = 0.9
beta_second = 0.95
adam_epsilon = 1e-08
learn_rate = 0.0003
weight_decay = 0.1

def frequencies(freq_bins):
    pairs = jnp.arange(HD // 2).astype(jnp.float32)
    theta = jnp.exp(pairs * (-2.0 * math.log(rope_base) / HD))
    gamma = freq_bins.astype(jnp.float32) / BINS
    return theta * ((1.0 - gamma) / yarn_factor + gamma)

def rotate(vectors, cosine, sine):
    half = vectors.shape[-1] // 2
    first = vectors[..., :half]
    second = vectors[..., half:]
    cosine = cosine[:, None, :]
    sine = sine[:, None, :]
    return jnp.concatenate([first * cosine - second * sine, second * cosine + first * sine], axis=-1)

def unrotate(vectors, cosine, sine):
    half = vectors.shape[-1] // 2
    first = vectors[..., :half]
    second = vectors[..., half:]
    cosine = cosine[:, None, :]
    sine = sine[:, None, :]
    return jnp.concatenate([first * cosine + second * sine, second * cosine - first * sine], axis=-1)

def reference(layer_input, queries, keys, values, out_grad, doc_ids, freq_bins, master, moment1, moment2):
    frequency = frequencies(freq_bins)
    positions = jnp.arange(LEN).astype(jnp.int32)
    angles = positions.astype(jnp.float32)[:, None] * frequency[None, :]
    cosine = jnp.cos(angles)
    sine = jnp.sin(angles)
    group_size = HQ // HK
    inv_root = 1.0 / math.sqrt(HD)

    def one_sequence(pieces):
        query_seq, key_seq, value_seq, grad_seq, doc_seq = pieces
        rot_q = (rotate(query_seq.reshape(LEN, HQ, HD).astype(jnp.float32), cosine, sine) * magnitude_scale).astype(jnp.bfloat16)
        rot_k = (rotate(key_seq.reshape(LEN, HK, HD).astype(jnp.float32), cosine, sine) * magnitude_scale).astype(jnp.bfloat16)
        value_heads = value_seq.reshape(LEN, HK, HD)
        grad_heads = grad_seq.reshape(LEN, HQ, HD)
        allowed = (positions[None, :] <= positions[:, None]) & (doc_seq[None, :] == doc_seq[:, None])
        query_parts = []
        key_parts = []
        value_parts = []
        for head in range(HK):
            query_head = rot_q[:, head * group_size:(head + 1) * group_size, :].astype(jnp.float32)
            grad_head = grad_heads[:, head * group_size:(head + 1) * group_size, :].astype(jnp.float32)
            key_head = rot_k[:, head, :].astype(jnp.float32)
            value_head = value_heads[:, head, :].astype(jnp.float32)
            scores = jnp.einsum('lgd,md->lgm', query_head, key_head) * inv_root
            scores = jnp.where(allowed[:, None, :], scores, -jnp.inf)
            row_max = lax.optimization_barrier(jnp.max(scores, axis=-1, keepdims=True))
            log_total = row_max + jnp.log(lax.optimization_barrier(jnp.sum(jnp.exp(scores - row_max), axis=-1, keepdims=True)))
            probs = jnp.exp(scores - log_total)
            prob_grad = jnp.einsum('lgd,md->lgm', grad_head, value_head)
            delta = lax.optimization_barrier(jnp.sum(probs * prob_grad, axis=-1, keepdims=True))
            score_grad = (probs * (prob_grad - delta) * inv_root).astype(jnp.bfloat16).astype(jnp.float32)
            probs_bf = probs.astype(jnp.bfloat16).astype(jnp.float32)
            query_parts.append(jnp.einsum('lgm,md->lgd', score_grad, key_head))
            key_parts.append(jnp.einsum('lgm,lgd->md', score_grad, query_head))
            value_parts.append(jnp.einsum('lgm,lgd->md', probs_bf, grad_head))
        rot_q_grad = jnp.concatenate(query_parts, axis=1)
        rot_k_grad = jnp.stack(key_parts, axis=1)
        value_grad = jnp.stack(value_parts, axis=1).astype(jnp.bfloat16).reshape(LEN, HK * HD)
        query_grad = (unrotate(rot_q_grad, cosine, sine) * magnitude_scale).astype(jnp.bfloat16).reshape(LEN, HQ * HD)
        key_grad = (unrotate(rot_k_grad, cosine, sine) * magnitude_scale).astype(jnp.bfloat16).reshape(LEN, HK * HD)
        return (query_grad, value_grad, key_grad)
    query_grad, value_grad, key_grad = lax.map(one_sequence, (queries, keys, values, out_grad, doc_ids))
    gradient = lax.dot_general(layer_input.reshape(SEQS * LEN, D), key_grad.reshape(SEQS * LEN, HK * HD), (((0,), (0,)), ((), ())), preferred_element_type=jnp.float32)
    gradient = gradient * (1.0 / math.sqrt(SEQS * LEN))
    gradient = gradient.reshape(ROW_GROUPS, D // ROW_GROUPS, HK * HD)
    new_moment1 = beta_first * moment1 + (1.0 - beta_first) * gradient
    new_moment2 = beta_second * moment2 + (1.0 - beta_second) * gradient * gradient
    first_fix = 1.0 - beta_first ** ADAM_STEP
    second_fix = 1.0 - beta_second ** ADAM_STEP
    update = new_moment1 / first_fix / (jnp.sqrt(new_moment2 / second_fix) + adam_epsilon)
    new_master = master - learn_rate * (update + weight_decay * master)
    key_weight = new_master.astype(jnp.bfloat16)
    return (query_grad, value_grad, new_master, new_moment1, new_moment2, key_weight)
```

```python
import functools
import math

import jax
import jax.numpy as jnp
from jax import lax
from jax.experimental import pallas as pl
from jax.experimental.pallas import tpu as pltpu
from jax.sharding import PartitionSpec as P

HD = 128
BINS = 32
ADAM_STEP = 10
NCTX = 8
NDP = 16
NZ = 8
NPLANE = 16
BACK = 4
LOC = 256
GROUP = 8
KVH = 2
WIN = (BACK + 1) * LOC
CH = 128

rope_base = 10000.0
yarn_factor = 8.0
magnitude_scale = 0.1 * math.log(8.0) + 1.0
beta_first = 0.9
beta_second = 0.95
adam_epsilon = 1e-08
learn_rate = 0.0003
weight_decay = 0.1
inv_root = 1.0 / math.sqrt(HD)
MESH = pl.DeviceIdType.MESH
F32 = jnp.float32
BF16 = jnp.bfloat16


def frequencies(freq_bins):
    pairs = jnp.arange(HD // 2).astype(jnp.float32)
    theta = jnp.exp(pairs * (-2.0 * math.log(rope_base) / HD))
    gamma = freq_bins.astype(jnp.float32) / BINS
    return theta * ((1.0 - gamma) / yarn_factor + gamma)


def dot_nt(a, b):
    return lax.dot_general(a, b, (((1,), (1,)), ((), ())), preferred_element_type=F32)


def dot_nn(a, b):
    return lax.dot_general(a, b, (((1,), (0,)), ((), ())), preferred_element_type=F32)


def rows8(op, value):
    return op(value.reshape(value.shape[0] // 8, 8, value.shape[1]), axis=0)


def kernel(
    q_hbm, og_hbm, k_ref, v_ref, doc_ref, cos_ref, sin_ref, x_hbm, ms_hbm, m1_hbm, m2_hbm,
    dq_hbm, dv_out, nms_out, nm1_out, nm2_out, kw_hbm,
    q_v, og_v, dq_v, kv, kt, docs, bias, t_ref, dp_ref, p_ref, ds_ref, dk_acc, dv_acc,
    term_send, term_recv, kg_own, dv_own, xr, kgt, gtb, rbuf, gall, opt_v, wb,
    local_sem, doc_send_sem, doc_recv_sem, kv_send_sem, kv_recv_sem, x_send_sem, x_recv_sem,
    xf_send_sem, xf_recv_sem, term_send_sem, term_recv_sem, kg_send_sem, kg_recv_sem,
    rs_send_sem, rs_recv_sem, ga_send_sem, ga_recv_sem,
    sw_send_sem, sw_recv_sem, ring_send_sem, ring_recv_sem,
    zs_send_sem, zs_recv_sem, pl_send_sem, pl_recv_sem,
):
    c = lax.axis_index("ctx")
    d = lax.axis_index("dp")
    t = lax.axis_index("tp")
    z = lax.rem(d, NZ)
    xl = d // NZ
    me_p = xl * NCTX + c

    def z_peer(k):
        return (c, xl * NZ + lax.rem(z + k, NZ), t)

    def plane_peer(k):
        p = lax.rem(me_p + k, NPLANE)
        return p, (lax.rem(p, NCTX), (p // NCTX) * NZ + z, t)

    def ctx_peer(k):
        return (lax.rem(c + k, NCTX), d, t)

    def remote(src, dst, ssem, rsem, device):
        return pltpu.make_async_remote_copy(
            src_ref=src, dst_ref=dst, send_sem=ssem, recv_sem=rsem,
            device_id=device, device_id_type=MESH,
        )

    q_copy = pltpu.make_async_copy(q_hbm, q_v, local_sem.at[0])
    og_copy = pltpu.make_async_copy(og_hbm, og_v, local_sem.at[1])
    opt_copies = [
        pltpu.make_async_copy(src, opt_v.at[i], local_sem.at[2 + i])
        for i, src in enumerate((ms_hbm, m1_hbm, m2_hbm))
    ]
    x_own = [
        pltpu.make_async_copy(
            x_hbm.at[:, pl.ds(pl.multiple_of((i * NZ + z) * LOC, LOC), LOC)],
            xr.at[t, i, pl.ds(pl.multiple_of(z * LOC, LOC), LOC), :],
            local_sem.at[5 + i],
        )
        for i in range(2)
    ]
    for copy in [q_copy, og_copy] + opt_copies + x_own:
        copy.start()

    barrier = pltpu.get_barrier_semaphore()

    def greet_z(k, carry):
        pl.semaphore_signal(barrier, inc=1, device_id=z_peer(k), device_id_type=MESH)
        return carry

    def greet_plane(k, carry):
        pl.semaphore_signal(barrier, inc=1, device_id=plane_peer(k)[1], device_id_type=MESH)
        return carry

    lax.fori_loop(1, NZ, greet_z, 0)
    lax.fori_loop(1, NPLANE, greet_plane, 0)
    pl.semaphore_signal(barrier, inc=1, device_id=(c, d, 1 - t), device_id_type=MESH)

    cosv = cos_ref[...]
    sinv = sin_ref[...]
    for g in range(KVH):
        kh = k_ref[:, g * HD:(g + 1) * HD].astype(F32)
        kv[g, 0, 0:LOC, :] = (kh * cosv + pltpu.roll(kh, HD // 2, 1) * sinv).astype(BF16)
        kv[g, 1, 0:LOC, :] = v_ref[:, g * HD:(g + 1) * HD]
    docs[0] = jnp.broadcast_to(doc_ref[...], (8, LOC))

    pl.semaphore_wait(barrier, (NZ - 1) + (NPLANE - 1) + 1)

    def doc_copy(k):
        return remote(docs.at[0], docs.at[k], doc_send_sem.at[k - 1], doc_recv_sem.at[k - 1], ctx_peer(k))

    def kv_copy(g, k):
        return remote(
            kv.at[g, :, pl.ds(0, LOC), :], kv.at[g, :, pl.ds(k * LOC, LOC), :],
            kv_send_sem.at[g, k - 1], kv_recv_sem.at[g, k - 1], ctx_peer(k),
        )

    for k in range(1, BACK + 1):
        @pl.when(c + k < NCTX)
        def _(k=k):
            doc_copy(k).start()
            kv_copy(0, k).start()

    def x_copy(k, i):
        zd = lax.rem(z + k, NZ)
        return remote(
            x_hbm.at[:, pl.ds(pl.multiple_of((i * NZ + zd) * LOC, LOC), LOC)],
            xr.at[t, i, pl.ds(pl.multiple_of(z * LOC, LOC), LOC), :],
            x_send_sem.at[k, i], x_recv_sem.at[k, i], z_peer(k),
        )

    def x_start(k, carry):
        x_copy(k, 0).start()
        x_copy(k, 1).start()
        return carry

    lax.fori_loop(1, NZ, x_start, 0)

    for k in range(1, BACK + 1):
        @pl.when(c + k < NCTX)
        def _(k=k):
            kv_copy(1, k).start()

        @pl.when(c < k)
        def _(k=k):
            kv[:, :, k * LOC:(k + 1) * LOC, :] = jnp.zeros((KVH, 2, LOC, HD), BF16)
            docs[k] = jnp.full((8, LOC), 127, jnp.int32)

    for k in range(1, BACK + 1):
        @pl.when(c >= k)
        def _(k=k):
            doc_copy(k).wait_recv()
    own_docs = doc_ref[...]
    window_start = jnp.maximum(c - BACK, 0) * LOC
    start = jnp.zeros((1, LOC), F32)
    for doc in range(1, 4):
        below = jnp.zeros((8, LOC), F32)
        for k in range(BACK + 1):
            below = below + (docs[k] < doc).astype(F32)
        count = jnp.sum(below[0:1], axis=1, keepdims=True)
        start = jnp.where(own_docs == doc, count, start)
    start = start.astype(jnp.int32) + window_start
    query_pos = c * LOC + lax.broadcasted_iota(jnp.int32, (1, LOC), 1)
    for k in range(BACK + 1):
        key_pos = (c - k) * LOC + lax.broadcasted_iota(jnp.int32, (LOC, LOC), 0)
        seen = (key_pos <= query_pos) & (key_pos >= start)
        bias[k * LOC:(k + 1) * LOC, :] = jnp.where(seen, 0.0, -jnp.inf)

    q_copy.wait()
    og_copy.wait()
    scale2 = inv_root * math.log2(math.e)
    chunks = [slice(j * CH, (j + 1) * CH) for j in range(WIN // CH)]

    def term_copy(g, kind, k):
        return remote(
            term_send.at[g, kind, k - 1], term_recv.at[g, kind, k - 1],
            term_send_sem.at[g, kind, k - 1], term_recv_sem.at[g, kind, k - 1],
            ctx_peer(NCTX - k),
        )

    for g in range(KVH):
        for k in range(1, BACK + 1):
            @pl.when(c >= k)
            def _(k=k, g=g):
                kv_copy(g, k).wait_recv()
        for sl in chunks:
            kt[:, sl] = kv[g, 0, sl, :].astype(F32).T.astype(BF16)
        dk_acc[...] = jnp.zeros_like(dk_acc)
        dv_acc[...] = jnp.zeros_like(dv_acc)

        def one_head(h, carry, g=g):
            col = pl.ds(pl.multiple_of((g * GROUP + h) * HD, HD), HD)
            qh = q_v[:, col].astype(F32)
            rq = (qh * cos_ref[...] + pltpu.roll(qh, HD // 2, 1) * sin_ref[...]).astype(BF16)
            do = og_v[:, col]
            top = None
            for sl in chunks:
                score = dot_nt(kv[g, 0, sl, :], rq) * scale2 + bias[sl, :]
                t_ref[sl, :] = score
                part = rows8(jnp.max, score)
                top = part if top is None else jnp.maximum(top, part)
            top = jnp.max(top, axis=0, keepdims=True)
            total = jnp.zeros((8, LOC), F32)
            mixed = jnp.zeros((8, LOC), F32)
            for sl in chunks:
                e = jnp.exp2(t_ref[sl, :] - top)
                t_ref[sl, :] = e
                dp = dot_nt(kv[g, 1, sl, :], do)
                dp_ref[sl, :] = dp
                total = total + rows8(jnp.sum, e)
                mixed = mixed + rows8(jnp.sum, e * dp)
            inv_total = 1.0 / jnp.sum(total, axis=0, keepdims=True)
            delta = jnp.sum(mixed, axis=0, keepdims=True) * inv_total
            for sl in chunks:
                p = t_ref[sl, :] * inv_total
                ds = (p * (dp_ref[sl, :] - delta)).astype(BF16)
                ds_ref[sl, :] = ds
                dk_acc[sl, :] += dot_nn(ds, rq)
                dv_acc[sl, :] += dot_nn(p.astype(BF16), do)
            dq = dot_nn(kt[...], ds_ref[...]).T * inv_root
            dq_v[:, col] = (dq * cos_ref[...] - pltpu.roll(dq, HD // 2, 1) * sin_ref[...]).astype(BF16)
            return carry

        lax.fori_loop(0, GROUP, one_head, 0)

        kg_own[g] = dk_acc[0:LOC, :] * inv_root
        dv_own[g] = dv_acc[0:LOC, :]
        for k in range(1, BACK + 1):
            rows = slice(k * LOC, (k + 1) * LOC)
            term_send[g, 0, k - 1] = (dk_acc[rows, :] * inv_root).astype(BF16)
            term_send[g, 1, k - 1] = dv_acc[rows, :].astype(BF16)
        for kind in range(2):
            for k in range(1, BACK + 1):
                @pl.when(c >= k)
                def _(k=k, g=g, kind=kind):
                    term_copy(g, kind, k).start()

    dq_copy = pltpu.make_async_copy(dq_v, dq_hbm, local_sem.at[7])
    dq_copy.start()

    def kg_copy(g, k):
        part = kgt.at[z, pl.ds(g * HD, HD), :]
        return remote(part, part, kg_send_sem.at[g, k], kg_recv_sem.at[g, k], z_peer(k))

    for g in range(KVH):
        for k in range(1, BACK + 1):
            @pl.when(c + k < NCTX)
            def _(k=k, g=g):
                term_copy(g, 0, k).wait_recv()
                kg_own[g] = kg_own[g] + term_recv[g, 0, k - 1].astype(F32)
        kg = kg_own[g]
        kg = kg * cosv - pltpu.roll(kg, HD // 2, 1) * sinv
        kgt[z, pl.ds(g * HD, HD), :] = kg.T.astype(BF16)

        def kg_start(k, carry, g=g):
            kg_copy(g, k).start()
            return carry

        lax.fori_loop(1, NZ, kg_start, 0)

    for copy in x_own:
        copy.wait()

    def x_wait(k, carry):
        x_copy(k, 0).wait_recv()
        x_copy(k, 1).wait_recv()
        return carry

    lax.fori_loop(1, NZ, x_wait, 0)
    xf_copy = remote(xr.at[t], xr.at[t], xf_send_sem, xf_recv_sem, (c, d, 1 - t))
    xf_copy.start()

    for g in range(KVH):
        for k in range(1, BACK + 1):
            @pl.when(c + k < NCTX)
            def _(k=k, g=g):
                term_copy(g, 1, k).wait_recv()
                dv_own[g] = dv_own[g] + term_recv[g, 1, k - 1].astype(F32)
        dv_out[:, g * HD:(g + 1) * HD] = dv_own[g].astype(BF16)

    def kg_wait(k, carry):
        kg_copy(0, k).wait_recv()
        kg_copy(1, k).wait_recv()
        return carry

    lax.fori_loop(1, NZ, kg_wait, 0)
    xf_copy.wait_recv()

    for i in range(2):
        for h in range(2):
            acc = jnp.zeros((LOC, LOC), F32)
            for s in range(NZ):
                acc = acc + dot_nn(kgt[s], xr[h, i, s * LOC:(s + 1) * LOC, :])
            gtb[i, :, h * LOC:(h + 1) * LOC] = acc.astype(BF16)

    part_rows = LOC // NCTX

    def rs_copy(k):
        p, device = plane_peer(k)
        return remote(
            gtb.at[p // NCTX, pl.ds(pl.multiple_of(lax.rem(p, NCTX) * part_rows, part_rows), part_rows), :],
            rbuf.at[k], rs_send_sem.at[k], rs_recv_sem.at[k], device,
        )

    def rs_start(k, carry):
        rs_copy(k).start()
        return carry

    lax.fori_loop(1, NPLANE, rs_start, 0)

    def rs_sum(k, total):
        rs_copy(k).wait_recv()
        return total + rbuf[k].astype(F32)

    own_rows = pl.ds(pl.multiple_of(c * part_rows, part_rows), part_rows)
    total = lax.fori_loop(1, NPLANE, rs_sum, gtb[xl, own_rows, :].astype(F32))
    gall[own_rows, :] = (total * (1.0 / math.sqrt(NDP * NCTX * LOC))).astype(BF16)

    def ga_copy(k):
        return remote(gall.at[own_rows, :], gall.at[own_rows, :], ga_send_sem.at[k], ga_recv_sem.at[k], ctx_peer(k))

    def ga_start(k, carry):
        ga_copy(k).start()
        return carry

    def ga_wait(k, carry):
        ga_copy(k).wait_recv()
        return carry

    lax.fori_loop(1, NCTX, ga_start, 0)
    for copy in opt_copies:
        copy.wait()
    lax.fori_loop(1, NCTX, ga_wait, 0)

    first_fix = 1.0 - beta_first**ADAM_STEP
    second_fix = 1.0 - beta_second**ADAM_STEP
    for h in range(2):
        grad = gall[:, h * LOC:(h + 1) * LOC].astype(F32).T
        nm1 = beta_first * opt_v[1, h] + (1.0 - beta_first) * grad
        nm2 = beta_second * opt_v[2, h] + (1.0 - beta_second) * grad * grad
        update = nm1 / first_fix / (jnp.sqrt(nm2 / second_fix) + adam_epsilon)
        nms = opt_v[0, h] - learn_rate * (update + weight_decay * opt_v[0, h])
        nms_out[h] = nms
        nm1_out[h] = nm1
        nm2_out[h] = nm2
        wb[h] = nms.astype(BF16).reshape(NCTX, part_rows, LOC)

    keeps = [
        pltpu.make_async_copy(wb.at[0], kw_hbm.at[0, d], local_sem.at[8]),
        pltpu.make_async_copy(wb.at[1, c], kw_hbm.at[1, d, c], local_sem.at[9]),
    ]
    for keep in keeps:
        keep.start()

    def zs_copy(k):
        return remote(
            wb.at[1, c], kw_hbm.at[1, d, c], zs_send_sem.at[k], zs_recv_sem.at[k], z_peer(k),
        )

    swap = remote(wb.at[0], kw_hbm.at[0, d], sw_send_sem, sw_recv_sem, (c, (1 - xl) * NZ + z, t))

    def ring_copy(s, way, same, src=None):
        step = 1 if way == 0 else NZ - 1
        zb = lax.rem(z + (NZ - s if way == 0 else s), NZ)
        block = (xl if same else 1 - xl) * NZ + zb
        return remote(
            kw_hbm.at[0, block] if src is None else src, kw_hbm.at[0, block],
            ring_send_sem.at[way, s, int(same)], ring_recv_sem.at[way, s, int(same)], z_peer(step),
        )

    def zs_start(k, carry):
        zs_copy(k).start()
        return carry

    swap.start()
    ring_copy(0, 0, True, wb.at[0]).start()
    ring_copy(0, 1, True, wb.at[0]).start()
    lax.fori_loop(1, NZ, zs_start, 0)

    def zs_wait(k, carry):
        zs_copy(k).wait_recv()
        return carry

    swap.wait_recv()
    ring_copy(0, 0, False).start()
    ring_copy(0, 1, False).start()
    lax.fori_loop(1, NZ, zs_wait, 0)
    for keep in keeps:
        keep.wait()

    def pl_copy(k):
        device = plane_peer(k)[1]
        part = kw_hbm.at[1, pl.ds(xl * NZ, NZ), c]
        return remote(part, part, pl_send_sem.at[k], pl_recv_sem.at[k], device)

    def pl_start(k, carry):
        pl_copy(k).start()
        return carry

    lax.fori_loop(1, NPLANE, pl_start, 0)

    ring = [(s, way, same) for s in range(4) for same in (True, False) for way in range(2) if s < 3 or same == (way == 0)]
    for s, way, same in ring:
        ring_copy(s, way, same).wait_recv()
        if (s + 1, way, same) in ring:
            ring_copy(s + 1, way, same).start()

    def pl_wait(k, carry):
        pl_copy(k).wait_recv()
        return carry

    lax.fori_loop(1, NPLANE, pl_wait, 0)

    for k in range(1, BACK + 1):
        @pl.when(c + k < NCTX)
        def _(k=k):
            doc_copy(k).wait_send()
            for g in range(KVH):
                kv_copy(g, k).wait_send()

        @pl.when(c >= k)
        def _(k=k):
            for g in range(KVH):
                for kind in range(2):
                    term_copy(g, kind, k).wait_send()

    def z_sent(k, carry):
        x_copy(k, 0).wait_send()
        x_copy(k, 1).wait_send()
        kg_copy(0, k).wait_send()
        kg_copy(1, k).wait_send()
        zs_copy(k).wait_send()
        return carry

    lax.fori_loop(1, NZ, z_sent, 0)

    def plane_sent(k, carry):
        rs_copy(k).wait_send()
        pl_copy(k).wait_send()
        return carry

    lax.fori_loop(1, NPLANE, plane_sent, 0)

    def ctx_sent(k, carry):
        ga_copy(k).wait_send()
        return carry

    lax.fori_loop(1, NCTX, ctx_sent, 0)
    xf_copy.wait_send()
    swap.wait_send()
    for s, way, same in ring:
        ring_copy(s, way, same).wait_send()
    dq_copy.wait()


def on_device(
    layer_input, queries, keys, values, out_grad, doc_ids, freq_bins, master, moment1, moment2
):
    positions = lax.axis_index("ctx") * LOC + jnp.arange(LOC, dtype=jnp.int32)
    angles = positions.astype(F32)[:, None] * frequencies(freq_bins)[None, :]
    cosine = jnp.cos(angles) * magnitude_scale
    sine = jnp.sin(angles) * magnitude_scale
    cosine = jnp.concatenate([cosine, cosine], axis=1)
    sine = jnp.concatenate([-sine, sine], axis=1)

    any_ = pl.BlockSpec(memory_space=pl.ANY)
    vmem = pl.BlockSpec(memory_space=pltpu.VMEM)
    dma = pltpu.SemaphoreType.DMA
    part_rows = LOC // NCTX
    rows, cols = 2, LOC
    state = jax.ShapeDtypeStruct((rows, LOC, cols), F32)
    dq, dv, nms, nm1, nm2, kw = pl.pallas_call(
        kernel,
        out_shape=(
            jax.ShapeDtypeStruct((LOC, KVH * GROUP * HD), BF16),
            jax.ShapeDtypeStruct((LOC, KVH * HD), BF16),
            state, state, state,
            jax.ShapeDtypeStruct((2, NDP, NCTX, part_rows, cols), BF16),
        ),
        in_specs=[any_, any_, vmem, vmem, vmem, vmem, vmem, any_, any_, any_, any_],
        out_specs=(any_, vmem, vmem, vmem, vmem, any_),
        scratch_shapes=[
            pltpu.VMEM((LOC, KVH * GROUP * HD), BF16),
            pltpu.VMEM((LOC, KVH * GROUP * HD), BF16),
            pltpu.VMEM((LOC, KVH * GROUP * HD), BF16),
            pltpu.VMEM((KVH, 2, WIN, HD), BF16),
            pltpu.VMEM((HD, WIN), BF16),
            pltpu.VMEM((BACK + 1, 8, LOC), jnp.int32),
            pltpu.VMEM((WIN, LOC), F32),
            pltpu.VMEM((WIN, LOC), F32),
            pltpu.VMEM((WIN, LOC), F32),
            pltpu.VMEM((WIN, LOC), BF16),
            pltpu.VMEM((WIN, LOC), BF16),
            pltpu.VMEM((WIN, HD), F32),
            pltpu.VMEM((WIN, HD), F32),
            pltpu.VMEM((KVH, 2, BACK, LOC, HD), BF16),
            pltpu.VMEM((KVH, 2, BACK, LOC, HD), BF16),
            pltpu.VMEM((KVH, LOC, HD), F32),
            pltpu.VMEM((KVH, LOC, HD), F32),
            pltpu.VMEM((2, 2, NZ * LOC, LOC), BF16),
            pltpu.VMEM((NZ, LOC, LOC), BF16),
            pltpu.VMEM((2, LOC, 2 * LOC), BF16),
            pltpu.VMEM((NPLANE, part_rows, 2 * LOC), BF16),
            pltpu.VMEM((LOC, 2 * LOC), BF16),
            pltpu.VMEM((3, 2, LOC, LOC), F32),
            pltpu.VMEM((2, NCTX, part_rows, LOC), BF16),
            dma((10,)),
            dma((BACK,)), dma((BACK,)),
            dma((KVH, BACK)), dma((KVH, BACK)),
            dma((NZ, 2)), dma((NZ, 2)),
            dma, dma,
            dma((KVH, 2, BACK)), dma((KVH, 2, BACK)),
            dma((KVH, NZ)), dma((KVH, NZ)),
            dma((NPLANE,)), dma((NPLANE,)),
            dma((NCTX,)), dma((NCTX,)),
            dma, dma,
            dma((2, 4, 2)), dma((2, 4, 2)),
            dma((NZ,)), dma((NZ,)),
            dma((NPLANE,)), dma((NPLANE,)),
        ],
        compiler_params=pltpu.CompilerParams(
            collective_id=0, has_side_effects=True, vmem_limit_bytes=48 * 1024 * 1024
        ),
    )(
        queries[0], out_grad[0], keys[0], values[0], doc_ids, cosine, sine, layer_input[0],
        master, moment1, moment2,
    )
    return (dq[None], dv[None], nms, nm1, nm2, kw.reshape(2, NDP * LOC, cols))


def solution(mesh):
    placed = (
        P("dp", "ctx", "tp"),
        P("dp", "ctx", "tp"),
        P("dp", "ctx", "tp"),
        P("dp", "ctx", "tp"),
        P("dp", "ctx", "tp"),
        P("dp", "ctx"),
        P(),
        P(None, "dp", "tp"),
        P(None, "dp", "tp"),
        P(None, "dp", "tp"),
    )
    return jax.shard_map(
        on_device,
        mesh=mesh,
        in_specs=placed,
        out_specs=(
            P("dp", "ctx", "tp"),
            P("dp", "ctx", "tp"),
            P(None, "dp", "tp"),
            P(None, "dp", "tp"),
            P(None, "dp", "tp"),
            P(None, None, "tp"),
        ),
        check_vma=False,
    )
```

```python
import functools
import math

import jax
import jax.numpy as jnp
from jax import lax
from jax.experimental import pallas as pl
from jax.experimental.pallas import tpu as pltpu
from jax.sharding import PartitionSpec as P

HD = 128
BINS = 32
ADAM_STEP = 10
NCTX = 8
NDP = 16
NZ = 8
NPLANE = 16
BACK = 4
LOC = 256
GROUP = 8
KVH = 2
WIN = (BACK + 1) * LOC
CH = 128

rope_base = 10000.0
yarn_factor = 8.0
magnitude_scale = 0.1 * math.log(8.0) + 1.0
beta_first = 0.9
beta_second = 0.95
adam_epsilon = 1e-08
learn_rate = 0.0003
weight_decay = 0.1
inv_root = 1.0 / math.sqrt(HD)
MESH = pl.DeviceIdType.MESH
F32 = jnp.float32
BF16 = jnp.bfloat16


def frequencies(freq_bins):
    pairs = jnp.arange(HD // 2).astype(jnp.float32)
    theta = jnp.exp(pairs * (-2.0 * math.log(rope_base) / HD))
    gamma = freq_bins.astype(jnp.float32) / BINS
    return theta * ((1.0 - gamma) / yarn_factor + gamma)


def dot_nt(a, b):
    return lax.dot_general(a, b, (((1,), (1,)), ((), ())), preferred_element_type=F32)


def dot_nn(a, b):
    return lax.dot_general(a, b, (((1,), (0,)), ((), ())), preferred_element_type=F32)


def adam(grad, master, moment1, moment2):
    new_moment1 = beta_first * moment1 + (1.0 - beta_first) * grad
    new_moment2 = beta_second * moment2 + (1.0 - beta_second) * grad * grad
    first_fix = 1.0 - beta_first**ADAM_STEP
    second_fix = 1.0 - beta_second**ADAM_STEP
    update = new_moment1 / first_fix / (jnp.sqrt(new_moment2 / second_fix) + adam_epsilon)
    return master - learn_rate * (update + weight_decay * master), new_moment1, new_moment2


def rows8(op, value):
    return op(value.reshape(value.shape[0] // 8, 8, value.shape[1]), axis=0)


def kernel(
    q_hbm, og_hbm, k_ref, v_ref, doc_ref, cos_ref, sin_ref, x_hbm, ms_hbm, m1_hbm, m2_hbm,
    dq_hbm, dv_out, grad_out, kw_hbm,
    q_v, og_v, dq_v, kv, kt, docs, bias, rq_ref, t_ref, dp_ref, p_ref, ds_ref, dk_acc, dv_acc,
    term_send, term_recv, kg_own, dv_own, xr, kgt, gtb, rbuf, gall, opt_v, wb,
    local_sem, doc_send_sem, doc_recv_sem, kv_send_sem, kv_recv_sem, x_send_sem, x_recv_sem,
    xf_send_sem, xf_recv_sem, term_send_sem, term_recv_sem, kg_send_sem, kg_recv_sem,
    rs_send_sem, rs_recv_sem, ga_send_sem, ga_recv_sem,
    sw_send_sem, sw_recv_sem, ring_send_sem, ring_recv_sem,
    zs_send_sem, zs_recv_sem, pl_send_sem, pl_recv_sem,
):
    c = lax.axis_index("ctx")
    d = lax.axis_index("dp")
    t = lax.axis_index("tp")
    z = lax.rem(d, NZ)
    xl = d // NZ
    me_p = xl * NCTX + c

    def z_peer(k):
        return (c, xl * NZ + lax.rem(z + k, NZ), t)

    def plane_peer(k):
        p = lax.rem(me_p + k, NPLANE)
        return p, (lax.rem(p, NCTX), (p // NCTX) * NZ + z, t)

    def ctx_peer(k):
        return (lax.rem(c + k, NCTX), d, t)

    def remote(src, dst, ssem, rsem, device):
        return pltpu.make_async_remote_copy(
            src_ref=src, dst_ref=dst, send_sem=ssem, recv_sem=rsem,
            device_id=device, device_id_type=MESH,
        )

    sent = []

    def over(low, high, one):
        def step(k, carry):
            one(k)
            return carry

        lax.fori_loop(low, high, step, 0)

    q_copy = pltpu.make_async_copy(q_hbm, q_v, local_sem.at[0])
    og_copy = pltpu.make_async_copy(og_hbm, og_v, local_sem.at[1])
    opt_copies = [
        pltpu.make_async_copy(src, opt_v.at[i], local_sem.at[2 + i])
        for i, src in enumerate((ms_hbm, m1_hbm, m2_hbm))
    ]
    x_own = [
        pltpu.make_async_copy(
            x_hbm.at[:, pl.ds(pl.multiple_of((i * NZ + z) * LOC, LOC), LOC)],
            xr.at[t, i, pl.ds(pl.multiple_of(z * LOC, LOC), LOC), :],
            local_sem.at[5 + i],
        )
        for i in range(2)
    ]
    for copy in [q_copy, og_copy] + opt_copies + x_own:
        copy.start()

    barrier = pltpu.get_barrier_semaphore()

    def greet_z(k, carry):
        pl.semaphore_signal(barrier, inc=1, device_id=z_peer(k), device_id_type=MESH)
        return carry

    def greet_plane(k, carry):
        pl.semaphore_signal(barrier, inc=1, device_id=plane_peer(k)[1], device_id_type=MESH)
        return carry

    lax.fori_loop(1, NZ, greet_z, 0)
    lax.fori_loop(1, NPLANE, greet_plane, 0)
    pl.semaphore_signal(barrier, inc=1, device_id=(c, d, 1 - t), device_id_type=MESH)

    cosv = cos_ref[...]
    sinv = sin_ref[...]
    for g in range(KVH):
        kh = k_ref[:, g * HD:(g + 1) * HD].astype(F32)
        kv[g, 0, 0:LOC, :] = (kh * cosv + pltpu.roll(kh, HD // 2, 1) * sinv).astype(BF16)
        kv[g, 1, 0:LOC, :] = v_ref[:, g * HD:(g + 1) * HD]
    docs[0] = jnp.broadcast_to(doc_ref[...], (8, LOC))

    pl.semaphore_wait(barrier, (NZ - 1) + (NPLANE - 1) + 1)

    def doc_copy(k):
        return remote(docs.at[0], docs.at[k], doc_send_sem.at[k - 1], doc_recv_sem.at[k - 1], ctx_peer(k))

    def kv_copy(g, k):
        return remote(
            kv.at[g, :, pl.ds(0, LOC), :], kv.at[g, :, pl.ds(k * LOC, LOC), :],
            kv_send_sem.at[g, k - 1], kv_recv_sem.at[g, k - 1], ctx_peer(k),
        )

    for k in range(1, BACK + 1):
        @pl.when(c + k < NCTX)
        def _(k=k):
            doc_copy(k).start()
            kv_copy(0, k).start()

    def kv_sent():
        for k in range(1, BACK + 1):
            @pl.when(c + k < NCTX)
            def _(k=k):
                doc_copy(k).wait_send()
                for g in range(KVH):
                    kv_copy(g, k).wait_send()

    sent.append(kv_sent)

    def x_copy(k, i):
        zd = lax.rem(z + k, NZ)
        return remote(
            x_hbm.at[:, pl.ds(pl.multiple_of((i * NZ + zd) * LOC, LOC), LOC)],
            xr.at[t, i, pl.ds(pl.multiple_of(z * LOC, LOC), LOC), :],
            x_send_sem.at[k, i], x_recv_sem.at[k, i], z_peer(k),
        )

    def x_start(k, carry):
        x_copy(k, 0).start()
        x_copy(k, 1).start()
        return carry

    def x_sent(k):
        x_copy(k, 0).wait_send()
        x_copy(k, 1).wait_send()

    sent.append(lambda: over(1, NZ, x_sent))

    lax.fori_loop(1, NZ, x_start, 0)

    for k in range(1, BACK + 1):
        @pl.when(c + k < NCTX)
        def _(k=k):
            kv_copy(1, k).start()

        @pl.when(c < k)
        def _(k=k):
            kv[:, :, k * LOC:(k + 1) * LOC, :] = jnp.zeros((KVH, 2, LOC, HD), BF16)
            docs[k] = jnp.full((8, LOC), 127, jnp.int32)

    for k in range(1, BACK + 1):
        @pl.when(c >= k)
        def _(k=k):
            doc_copy(k).wait_recv()
    own_docs = doc_ref[...]
    window_start = jnp.maximum(c - BACK, 0) * LOC
    start = jnp.zeros((1, LOC), F32)
    for doc in range(1, 4):
        below = jnp.zeros((8, LOC), F32)
        for k in range(BACK + 1):
            below = below + (docs[k] < doc).astype(F32)
        count = jnp.sum(below[0:1], axis=1, keepdims=True)
        start = jnp.where(own_docs == doc, count, start)
    start = start.astype(jnp.int32) + window_start
    query_pos = c * LOC + lax.broadcasted_iota(jnp.int32, (1, LOC), 1)
    for k in range(BACK + 1):
        key_pos = (c - k) * LOC + lax.broadcasted_iota(jnp.int32, (LOC, LOC), 0)
        seen = (key_pos <= query_pos) & (key_pos >= start)
        bias[k * LOC:(k + 1) * LOC, :] = jnp.where(seen, 0.0, -jnp.inf)

    q_copy.wait()
    og_copy.wait()
    scale2 = inv_root * math.log2(math.e)
    chunks = [slice(j * CH, (j + 1) * CH) for j in range(WIN // CH)]

    def term_copy(g, kind, k):
        return remote(
            term_send.at[g, kind, k - 1], term_recv.at[g, kind, k - 1],
            term_send_sem.at[g, kind, k - 1], term_recv_sem.at[g, kind, k - 1],
            ctx_peer(NCTX - k),
        )

    def term_sent(g):
        for k in range(1, BACK + 1):
            @pl.when(c >= k)
            def _(k=k):
                for kind in range(2):
                    term_copy(g, kind, k).wait_send()

    sent.append(lambda: term_sent(0))
    sent.append(lambda: term_sent(1))
    for g in range(KVH):
        for k in range(1, BACK + 1):
            @pl.when(c >= k)
            def _(k=k, g=g):
                kv_copy(g, k).wait_recv()
        for sl in chunks:
            kt[:, sl] = kv[g, 0, sl, :].astype(F32).T.astype(BF16)
        dk_acc[...] = jnp.zeros_like(dk_acc)
        dv_acc[...] = jnp.zeros_like(dv_acc)

        def head_columns(h, g=g):
            return pl.ds(pl.multiple_of((g * GROUP + h) * HD, HD), HD)

        def products(h, b, g=g):
            qh = q_v[:, head_columns(h)].astype(F32)
            rq = (qh * cos_ref[...] + pltpu.roll(qh, HD // 2, 1) * sin_ref[...]).astype(BF16)
            rq_ref[b] = rq
            t_ref[b] = dot_nt(kv[g, 0], rq)
            dp_ref[b] = dot_nt(kv[g, 1], og_v[:, head_columns(h)])

        def softmax(b):
            top = None
            for sl in chunks:
                score = t_ref[b, sl, :] * scale2 + bias[sl, :]
                t_ref[b, sl, :] = score
                part = rows8(jnp.max, score)
                top = part if top is None else jnp.maximum(top, part)
            top = jnp.max(top, axis=0, keepdims=True)
            total = jnp.zeros((8, LOC), F32)
            mixed = jnp.zeros((8, LOC), F32)
            for sl in chunks:
                e = jnp.exp2(t_ref[b, sl, :] - top)
                t_ref[b, sl, :] = e
                total = total + rows8(jnp.sum, e)
                mixed = mixed + rows8(jnp.sum, e * dp_ref[b, sl, :])
            inv_total = 1.0 / jnp.sum(total, axis=0, keepdims=True)
            delta = jnp.sum(mixed, axis=0, keepdims=True) * inv_total
            for sl in chunks:
                p = t_ref[b, sl, :] * inv_total
                ds_ref[b, sl, :] = (p * (dp_ref[b, sl, :] - delta)).astype(BF16)
                p_ref[b, sl, :] = p.astype(BF16)

        def gradients(h, b):
            dk_acc[...] += dot_nn(ds_ref[b], rq_ref[b])
            dv_acc[...] += dot_nn(p_ref[b], og_v[:, head_columns(h)])
            dq = dot_nn(kt[...], ds_ref[b]).T * inv_root
            dq = dq * cos_ref[...] - pltpu.roll(dq, HD // 2, 1) * sin_ref[...]
            dq_v[:, head_columns(h)] = dq.astype(BF16)

        def two_heads(i, carry):
            for b in range(2):
                products(2 * i + b, b)
            for b in range(2):
                softmax(b)
            for b in range(2):
                gradients(2 * i + b, b)
            return carry

        lax.fori_loop(0, GROUP // 2, two_heads, 0)

        kg_own[g] = dk_acc[0:LOC, :] * inv_root
        dv_own[g] = dv_acc[0:LOC, :]
        for k in range(1, BACK + 1):
            rows = slice(k * LOC, (k + 1) * LOC)
            term_send[g, 0, k - 1] = (dk_acc[rows, :] * inv_root).astype(BF16)
            term_send[g, 1, k - 1] = dv_acc[rows, :].astype(BF16)
        for kind in range(2):
            for k in range(1, BACK + 1):
                @pl.when(c >= k)
                def _(k=k, g=g, kind=kind):
                    term_copy(g, kind, k).start()

    dq_copy = pltpu.make_async_copy(dq_v, dq_hbm, local_sem.at[7])
    dq_copy.start()
    sent.append(dq_copy.wait)

    def kg_copy(s, way, g):
        zb = lax.rem(z + (NZ - s if way == 0 else s), NZ)
        part = kgt.at[zb, pl.ds(g * HD, HD), :]
        return remote(
            part, part, kg_send_sem.at[way, s, g], kg_recv_sem.at[way, s, g],
            z_peer(1 if way == 0 else NZ - 1),
        )

    kg_ring = [(s, way, g) for s in range(4) for g in range(KVH) for way in range(2) if s < 3 or g == way]
    for g in range(KVH):
        for k in range(1, BACK + 1):
            @pl.when(c + k < NCTX)
            def _(k=k, g=g):
                term_copy(g, 0, k).wait_recv()
                kg_own[g] = kg_own[g] + term_recv[g, 0, k - 1].astype(F32)
        kg = kg_own[g]
        kg = kg * cosv - pltpu.roll(kg, HD // 2, 1) * sinv
        kgt[z, pl.ds(g * HD, HD), :] = kg.T.astype(BF16)
        for way in range(2):
            kg_copy(0, way, g).start()

    def xf_copy(k):
        rows = pl.ds(pl.multiple_of(lax.rem(z + NZ - k, NZ) * LOC, LOC), LOC)
        part = xr.at[t, :, rows, :]
        return remote(part, part, xf_send_sem.at[k], xf_recv_sem.at[k], (c, d, 1 - t))

    def x_forward(k):
        if k == 0:
            for copy in x_own:
                copy.wait()
        else:
            x_copy(k, 0).wait_recv()
            x_copy(k, 1).wait_recv()
        xf_copy(k).start()

    for k in (0, 1, 7, 2, 6):
        x_forward(k)
    for s, way, g in kg_ring:
        kg_copy(s, way, g).wait_recv()
        if (s + 1, way, g) in kg_ring:
            kg_copy(s + 1, way, g).start()
    for k in (3, 5, 4):
        x_forward(k)
    sent.extend(kg_copy(s, way, g).wait_send for s, way, g in kg_ring)
    sent.append(lambda: over(0, NZ, lambda k: xf_copy(k).wait_send()))

    for g in range(KVH):
        for k in range(1, BACK + 1):
            @pl.when(c + k < NCTX)
            def _(k=k, g=g):
                term_copy(g, 1, k).wait_recv()
                dv_own[g] = dv_own[g] + term_recv[g, 1, k - 1].astype(F32)
        dv_out[:, g * HD:(g + 1) * HD] = dv_own[g].astype(BF16)

    def xf_wait(k):
        xf_copy(k).wait_recv()

    over(0, NZ, xf_wait)

    for i in range(2):
        for h in range(2):
            acc = jnp.zeros((LOC, LOC), F32)
            for s in range(NZ):
                acc = acc + dot_nn(kgt[s], xr[h, i, s * LOC:(s + 1) * LOC, :])
            gtb[i, :, h * LOC:(h + 1) * LOC] = acc.astype(BF16)

    part_rows = LOC // NCTX

    def rs_copy(k):
        p, device = plane_peer(k)
        return remote(
            gtb.at[p // NCTX, pl.ds(pl.multiple_of(lax.rem(p, NCTX) * part_rows, part_rows), part_rows), :],
            rbuf.at[k], rs_send_sem.at[k], rs_recv_sem.at[k], device,
        )

    def rs_start(k, carry):
        rs_copy(k).start()
        return carry

    lax.fori_loop(1, NPLANE, rs_start, 0)

    def rs_sum(k, total):
        rs_copy(k).wait_recv()
        return total + rbuf[k].astype(F32)

    sent.append(lambda: over(1, NPLANE, lambda k: rs_copy(k).wait_send()))
    own_rows = pl.ds(pl.multiple_of(c * part_rows, part_rows), part_rows)
    total = lax.fori_loop(1, NPLANE, rs_sum, gtb[xl, own_rows, :].astype(F32))
    gall[own_rows, :] = (total * (1.0 / math.sqrt(NDP * NCTX * LOC))).astype(BF16)

    def ga_copy(k):
        return remote(gall.at[own_rows, :], gall.at[own_rows, :], ga_send_sem.at[k], ga_recv_sem.at[k], ctx_peer(k))

    def ga_start(k, carry):
        ga_copy(k).start()
        return carry

    def ga_wait(k, carry):
        ga_copy(k).wait_recv()
        return carry

    lax.fori_loop(1, NCTX, ga_start, 0)
    for copy in opt_copies:
        copy.wait()
    lax.fori_loop(1, NCTX, ga_wait, 0)

    sent.append(lambda: over(1, NCTX, lambda k: ga_copy(k).wait_send()))
    for h in range(2):
        grad = gall[:, h * LOC:(h + 1) * LOC].astype(F32).T
        grad_out[h] = grad
        nms = adam(grad, opt_v[0, h], opt_v[1, h], opt_v[2, h])[0]
        wb[h] = nms.astype(BF16).reshape(NCTX, part_rows, LOC)

    keeps = [
        pltpu.make_async_copy(wb.at[0], kw_hbm.at[0, d], local_sem.at[8]),
        pltpu.make_async_copy(wb.at[1, c], kw_hbm.at[1, d, c], local_sem.at[9]),
    ]
    for keep in keeps:
        keep.start()

    def zs_copy(k):
        return remote(
            wb.at[1, c], kw_hbm.at[1, d, c], zs_send_sem.at[k], zs_recv_sem.at[k], z_peer(k),
        )

    swap = remote(wb.at[0], kw_hbm.at[0, d], sw_send_sem, sw_recv_sem, (c, (1 - xl) * NZ + z, t))

    def ring_copy(s, way, same, src=None):
        step = 1 if way == 0 else NZ - 1
        zb = lax.rem(z + (NZ - s if way == 0 else s), NZ)
        block = (xl if same else 1 - xl) * NZ + zb
        return remote(
            kw_hbm.at[0, block] if src is None else src, kw_hbm.at[0, block],
            ring_send_sem.at[way, s, int(same)], ring_recv_sem.at[way, s, int(same)], z_peer(step),
        )

    def zs_start(k, carry):
        zs_copy(k).start()
        return carry

    sent.append(swap.wait_send)
    sent.append(lambda: over(1, NZ, lambda k: zs_copy(k).wait_send()))
    swap.start()
    ring_copy(0, 0, True, wb.at[0]).start()
    ring_copy(0, 1, True, wb.at[0]).start()
    lax.fori_loop(1, NZ, zs_start, 0)

    def zs_wait(k, carry):
        zs_copy(k).wait_recv()
        return carry

    swap.wait_recv()
    ring_copy(0, 0, False).start()
    ring_copy(0, 1, False).start()
    lax.fori_loop(1, NZ, zs_wait, 0)
    for keep in keeps:
        keep.wait()

    def pl_copy(k):
        device = plane_peer(k)[1]
        part = kw_hbm.at[1, pl.ds(xl * NZ, NZ), c]
        return remote(part, part, pl_send_sem.at[k], pl_recv_sem.at[k], device)

    def pl_start(k, carry):
        pl_copy(k).start()
        return carry

    lax.fori_loop(1, NPLANE, pl_start, 0)

    sent.append(lambda: over(1, NPLANE, lambda k: pl_copy(k).wait_send()))
    ring = [(s, way, same) for s in range(4) for same in (True, False) for way in range(2) if s < 3 or same == (way == 0)]
    for s, way, same in ring:
        ring_copy(s, way, same).wait_recv()
        if (s + 1, way, same) in ring:
            ring_copy(s + 1, way, same).start()

    sent.extend(ring_copy(s, way, same).wait_send for s, way, same in ring)

    def pl_wait(k, carry):
        pl_copy(k).wait_recv()
        return carry

    lax.fori_loop(1, NPLANE, pl_wait, 0)

    for wait in sent:
        wait()


def on_device(
    layer_input, queries, keys, values, out_grad, doc_ids, freq_bins, master, moment1, moment2
):
    positions = lax.axis_index("ctx") * LOC + jnp.arange(LOC, dtype=jnp.int32)
    angles = positions.astype(F32)[:, None] * frequencies(freq_bins)[None, :]
    cosine = jnp.cos(angles) * magnitude_scale
    sine = jnp.sin(angles) * magnitude_scale
    cosine = jnp.concatenate([cosine, cosine], axis=1)
    sine = jnp.concatenate([-sine, sine], axis=1)

    any_ = pl.BlockSpec(memory_space=pl.ANY)
    vmem = pl.BlockSpec(memory_space=pltpu.VMEM)
    dma = pltpu.SemaphoreType.DMA
    part_rows = LOC // NCTX
    rows, cols = 2, LOC
    dq, dv, grad, kw = pl.pallas_call(
        kernel,
        out_shape=(
            jax.ShapeDtypeStruct((LOC, KVH * GROUP * HD), BF16),
            jax.ShapeDtypeStruct((LOC, KVH * HD), BF16),
            jax.ShapeDtypeStruct((rows, LOC, cols), F32),
            jax.ShapeDtypeStruct((2, NDP, NCTX, part_rows, cols), BF16),
        ),
        in_specs=[any_, any_, vmem, vmem, vmem, vmem, vmem, any_, any_, any_, any_],
        out_specs=(any_, vmem, vmem, any_),
        scratch_shapes=[
            pltpu.VMEM((LOC, KVH * GROUP * HD), BF16),
            pltpu.VMEM((LOC, KVH * GROUP * HD), BF16),
            pltpu.VMEM((LOC, KVH * GROUP * HD), BF16),
            pltpu.VMEM((KVH, 2, WIN, HD), BF16),
            pltpu.VMEM((HD, WIN), BF16),
            pltpu.VMEM((BACK + 1, 8, LOC), jnp.int32),
            pltpu.VMEM((WIN, LOC), F32),
            pltpu.VMEM((2, LOC, HD), BF16),
            pltpu.VMEM((2, WIN, LOC), F32),
            pltpu.VMEM((2, WIN, LOC), F32),
            pltpu.VMEM((2, WIN, LOC), BF16),
            pltpu.VMEM((2, WIN, LOC), BF16),
            pltpu.VMEM((WIN, HD), F32),
            pltpu.VMEM((WIN, HD), F32),
            pltpu.VMEM((KVH, 2, BACK, LOC, HD), BF16),
            pltpu.VMEM((KVH, 2, BACK, LOC, HD), BF16),
            pltpu.VMEM((KVH, LOC, HD), F32),
            pltpu.VMEM((KVH, LOC, HD), F32),
            pltpu.VMEM((2, 2, NZ * LOC, LOC), BF16),
            pltpu.VMEM((NZ, LOC, LOC), BF16),
            pltpu.VMEM((2, LOC, 2 * LOC), BF16),
            pltpu.VMEM((NPLANE, part_rows, 2 * LOC), BF16),
            pltpu.VMEM((LOC, 2 * LOC), BF16),
            pltpu.VMEM((3, 2, LOC, LOC), F32),
            pltpu.VMEM((2, NCTX, part_rows, LOC), BF16),
            dma((10,)),
            dma((BACK,)), dma((BACK,)),
            dma((KVH, BACK)), dma((KVH, BACK)),
            dma((NZ, 2)), dma((NZ, 2)),
            dma((NZ,)), dma((NZ,)),
            dma((KVH, 2, BACK)), dma((KVH, 2, BACK)),
            dma((2, 4, KVH)), dma((2, 4, KVH)),
            dma((NPLANE,)), dma((NPLANE,)),
            dma((NCTX,)), dma((NCTX,)),
            dma, dma,
            dma((2, 4, 2)), dma((2, 4, 2)),
            dma((NZ,)), dma((NZ,)),
            dma((NPLANE,)), dma((NPLANE,)),
        ],
        compiler_params=pltpu.CompilerParams(
            collective_id=0, has_side_effects=True, vmem_limit_bytes=54 * 1024 * 1024
        ),
    )(
        queries[0], out_grad[0], keys[0], values[0], doc_ids, cosine, sine, layer_input[0],
        master, moment1, moment2,
    )
    new_master, new_moment1, new_moment2 = adam(grad, master, moment1, moment2)
    return (dq[None], dv[None], new_master, new_moment1, new_moment2, kw.reshape(2, NDP * LOC, cols))


def solution(mesh):
    placed = (
        P("dp", "ctx", "tp"),
        P("dp", "ctx", "tp"),
        P("dp", "ctx", "tp"),
        P("dp", "ctx", "tp"),
        P("dp", "ctx", "tp"),
        P("dp", "ctx"),
        P(),
        P(None, "dp", "tp"),
        P(None, "dp", "tp"),
        P(None, "dp", "tp"),
    )
    return jax.shard_map(
        on_device,
        mesh=mesh,
        in_specs=placed,
        out_specs=(
            P("dp", "ctx", "tp"),
            P("dp", "ctx", "tp"),
            P(None, "dp", "tp"),
            P(None, "dp", "tp"),
            P(None, "dp", "tp"),
            P(None, None, "tp"),
        ),
        check_vma=False,
    )
```

```python
import functools
import math

import jax
import jax.numpy as jnp
from jax import lax
from jax.experimental import pallas as pl
from jax.experimental.pallas import tpu as pltpu
from jax.sharding import PartitionSpec as P

HD = 128
BINS = 32
ADAM_STEP = 10
NCTX = 8
NDP = 16
NZ = 8
NPLANE = 16
BACK = 4
LOC = 256
GROUP = 8
KVH = 2
WIN = (BACK + 1) * LOC
CH = 128

rope_base = 10000.0
yarn_factor = 8.0
magnitude_scale = 0.1 * math.log(8.0) + 1.0
beta_first = 0.9
beta_second = 0.95
adam_epsilon = 1e-08
learn_rate = 0.0003
weight_decay = 0.1
inv_root = 1.0 / math.sqrt(HD)
MESH = pl.DeviceIdType.MESH
F32 = jnp.float32
BF16 = jnp.bfloat16


def frequencies(freq_bins):
    pairs = jnp.arange(HD // 2).astype(jnp.float32)
    theta = jnp.exp(pairs * (-2.0 * math.log(rope_base) / HD))
    gamma = freq_bins.astype(jnp.float32) / BINS
    return theta * ((1.0 - gamma) / yarn_factor + gamma)


def dot_nt(a, b):
    return lax.dot_general(a, b, (((1,), (1,)), ((), ())), preferred_element_type=F32)


def dot_nn(a, b):
    return lax.dot_general(a, b, (((1,), (0,)), ((), ())), preferred_element_type=F32)


def adam(grad, master, moment1, moment2):
    new_moment1 = beta_first * moment1 + (1.0 - beta_first) * grad
    new_moment2 = beta_second * moment2 + (1.0 - beta_second) * grad * grad
    first_fix = 1.0 - beta_first**ADAM_STEP
    second_fix = 1.0 - beta_second**ADAM_STEP
    update = new_moment1 / first_fix / (jnp.sqrt(new_moment2 / second_fix) + adam_epsilon)
    return master - learn_rate * (update + weight_decay * master), new_moment1, new_moment2


def rows8(op, value):
    return op(value.reshape(value.shape[0] // 8, 8, value.shape[1]), axis=0)


def kernel(
    q_hbm, og_hbm, k_ref, v_ref, doc_ref, cos_ref, sin_ref, x_hbm, ms_hbm, m1_hbm, m2_hbm,
    dq_hbm, dv_out, grad_out, kw_hbm,
    q_v, og_v, dq_v, kv, kt, docs, bias, rq_ref, t_ref, dp_ref, p_ref, ds_ref, dk_acc, dv_acc,
    term_send, term_recv, kg_own, dv_own, xr, kgt, gacc, gtb, rbuf, gall, opt_v, wb,
    local_sem, doc_send_sem, doc_recv_sem, kv_send_sem, kv_recv_sem, x_send_sem, x_recv_sem,
    xf_send_sem, xf_recv_sem, term_send_sem, term_recv_sem, kg_send_sem, kg_recv_sem,
    rs_send_sem, rs_recv_sem, ga_send_sem, ga_recv_sem,
    sw_send_sem, sw_recv_sem, ring_send_sem, ring_recv_sem,
    zs_send_sem, zs_recv_sem, pl_send_sem, pl_recv_sem,
):
    c = lax.axis_index("ctx")
    d = lax.axis_index("dp")
    t = lax.axis_index("tp")
    z = lax.rem(d, NZ)
    xl = d // NZ
    me_p = xl * NCTX + c

    def z_peer(k):
        return (c, xl * NZ + lax.rem(z + k, NZ), t)

    def plane_peer(k):
        p = lax.rem(me_p + k, NPLANE)
        return p, (lax.rem(p, NCTX), (p // NCTX) * NZ + z, t)

    def ctx_peer(k):
        return (lax.rem(c + k, NCTX), d, t)

    def remote(src, dst, ssem, rsem, device):
        return pltpu.make_async_remote_copy(
            src_ref=src, dst_ref=dst, send_sem=ssem, recv_sem=rsem,
            device_id=device, device_id_type=MESH,
        )

    sent = []

    def over(low, high, one):
        def step(k, carry):
            one(k)
            return carry

        lax.fori_loop(low, high, step, 0)

    q_copy = pltpu.make_async_copy(q_hbm, q_v, local_sem.at[0])
    og_copy = pltpu.make_async_copy(og_hbm, og_v, local_sem.at[1])
    opt_copies = [
        pltpu.make_async_copy(src, opt_v.at[i], local_sem.at[2 + i])
        for i, src in enumerate((ms_hbm, m1_hbm, m2_hbm))
    ]
    x_own = [
        pltpu.make_async_copy(
            x_hbm.at[:, pl.ds(pl.multiple_of((i * NZ + z) * LOC, LOC), LOC)],
            xr.at[t, i, pl.ds(pl.multiple_of(z * LOC, LOC), LOC), :],
            local_sem.at[5 + i],
        )
        for i in range(2)
    ]
    for copy in [q_copy, og_copy] + opt_copies + x_own:
        copy.start()

    barrier = pltpu.get_barrier_semaphore()

    def greet_z(k, carry):
        pl.semaphore_signal(barrier, inc=1, device_id=z_peer(k), device_id_type=MESH)
        return carry

    def greet_plane(k, carry):
        pl.semaphore_signal(barrier, inc=1, device_id=plane_peer(k)[1], device_id_type=MESH)
        return carry

    lax.fori_loop(1, NZ, greet_z, 0)
    lax.fori_loop(1, NPLANE, greet_plane, 0)
    pl.semaphore_signal(barrier, inc=1, device_id=(c, d, 1 - t), device_id_type=MESH)

    cosv = cos_ref[...]
    sinv = sin_ref[...]
    for g in range(KVH):
        kh = k_ref[:, g * HD:(g + 1) * HD].astype(F32)
        kv[g, 0, 0:LOC, :] = (kh * cosv + pltpu.roll(kh, HD // 2, 1) * sinv).astype(BF16)
        kv[g, 1, 0:LOC, :] = v_ref[:, g * HD:(g + 1) * HD]
    docs[0] = jnp.broadcast_to(doc_ref[...], (8, LOC))

    pl.semaphore_wait(barrier, (NZ - 1) + (NPLANE - 1) + 1)

    def doc_copy(k):
        return remote(docs.at[0], docs.at[k], doc_send_sem.at[k - 1], doc_recv_sem.at[k - 1], ctx_peer(k))

    def kv_copy(g, k):
        return remote(
            kv.at[g, :, pl.ds(0, LOC), :], kv.at[g, :, pl.ds(k * LOC, LOC), :],
            kv_send_sem.at[g, k - 1], kv_recv_sem.at[g, k - 1], ctx_peer(k),
        )

    for k in range(1, BACK + 1):
        @pl.when(c + k < NCTX)
        def _(k=k):
            doc_copy(k).start()
            kv_copy(0, k).start()

    def kv_sent():
        for k in range(1, BACK + 1):
            @pl.when(c + k < NCTX)
            def _(k=k):
                doc_copy(k).wait_send()
                for g in range(KVH):
                    kv_copy(g, k).wait_send()

    sent.append(kv_sent)

    def x_copy(k, i):
        zd = lax.rem(z + k, NZ)
        return remote(
            x_hbm.at[:, pl.ds(pl.multiple_of((i * NZ + zd) * LOC, LOC), LOC)],
            xr.at[t, i, pl.ds(pl.multiple_of(z * LOC, LOC), LOC), :],
            x_send_sem.at[k, i], x_recv_sem.at[k, i], z_peer(k),
        )

    def x_start(k, carry):
        x_copy(k, 0).start()
        x_copy(k, 1).start()
        return carry

    def x_sent(k):
        x_copy(k, 0).wait_send()
        x_copy(k, 1).wait_send()

    sent.append(lambda: over(1, NZ, x_sent))

    lax.fori_loop(1, NZ, x_start, 0)

    for k in range(1, BACK + 1):
        @pl.when(c + k < NCTX)
        def _(k=k):
            kv_copy(1, k).start()

        @pl.when(c < k)
        def _(k=k):
            kv[:, :, k * LOC:(k + 1) * LOC, :] = jnp.zeros((KVH, 2, LOC, HD), BF16)
            docs[k] = jnp.full((8, LOC), 127, jnp.int32)

    for k in range(1, BACK + 1):
        @pl.when(c >= k)
        def _(k=k):
            doc_copy(k).wait_recv()
    own_docs = doc_ref[...]
    window_start = jnp.maximum(c - BACK, 0) * LOC
    start = jnp.zeros((1, LOC), F32)
    for doc in range(1, 4):
        below = jnp.zeros((8, LOC), F32)
        for k in range(BACK + 1):
            below = below + (docs[k] < doc).astype(F32)
        count = jnp.sum(below[0:1], axis=1, keepdims=True)
        start = jnp.where(own_docs == doc, count, start)
    start = start.astype(jnp.int32) + window_start
    query_pos = c * LOC + lax.broadcasted_iota(jnp.int32, (1, LOC), 1)
    for k in range(BACK + 1):
        key_pos = (c - k) * LOC + lax.broadcasted_iota(jnp.int32, (LOC, LOC), 0)
        seen = (key_pos <= query_pos) & (key_pos >= start)
        bias[k * LOC:(k + 1) * LOC, :] = jnp.where(seen, 0.0, -jnp.inf)

    q_copy.wait()
    og_copy.wait()
    scale2 = inv_root * math.log2(math.e)
    chunks = [slice(j * CH, (j + 1) * CH) for j in range(WIN // CH)]

    def term_copy(g, kind, k):
        return remote(
            term_send.at[g, kind, k - 1], term_recv.at[g, kind, k - 1],
            term_send_sem.at[g, kind, k - 1], term_recv_sem.at[g, kind, k - 1],
            ctx_peer(NCTX - k),
        )

    def term_sent(g):
        for k in range(1, BACK + 1):
            @pl.when(c >= k)
            def _(k=k):
                for kind in range(2):
                    term_copy(g, kind, k).wait_send()

    sent.append(lambda: term_sent(0))
    sent.append(lambda: term_sent(1))
    for g in range(KVH):
        for k in range(1, BACK + 1):
            @pl.when(c >= k)
            def _(k=k, g=g):
                kv_copy(g, k).wait_recv()
        for sl in chunks:
            kt[:, sl] = kv[g, 0, sl, :].astype(F32).T.astype(BF16)
        dk_acc[...] = jnp.zeros_like(dk_acc)
        dv_acc[...] = jnp.zeros_like(dv_acc)

        def head_columns(h, g=g):
            return pl.ds(pl.multiple_of((g * GROUP + h) * HD, HD), HD)

        def products(h, b, g=g):
            qh = q_v[:, head_columns(h)].astype(F32)
            rq = (qh * cos_ref[...] + pltpu.roll(qh, HD // 2, 1) * sin_ref[...]).astype(BF16)
            rq_ref[b] = rq
            t_ref[b] = dot_nt(kv[g, 0], rq)
            dp_ref[b] = dot_nt(kv[g, 1], og_v[:, head_columns(h)])

        def softmax(b):
            top = None
            for sl in chunks:
                score = t_ref[b, sl, :] * scale2 + bias[sl, :]
                t_ref[b, sl, :] = score
                part = rows8(jnp.max, score)
                top = part if top is None else jnp.maximum(top, part)
            top = jnp.max(top, axis=0, keepdims=True)
            total = jnp.zeros((8, LOC), F32)
            mixed = jnp.zeros((8, LOC), F32)
            for sl in chunks:
                e = jnp.exp2(t_ref[b, sl, :] - top)
                t_ref[b, sl, :] = e
                total = total + rows8(jnp.sum, e)
                mixed = mixed + rows8(jnp.sum, e * dp_ref[b, sl, :])
            inv_total = 1.0 / jnp.sum(total, axis=0, keepdims=True)
            delta = jnp.sum(mixed, axis=0, keepdims=True) * inv_total
            for sl in chunks:
                p = t_ref[b, sl, :] * inv_total
                ds_ref[b, sl, :] = (p * (dp_ref[b, sl, :] - delta)).astype(BF16)
                p_ref[b, sl, :] = p.astype(BF16)

        def gradients(h, b):
            dk_acc[...] += dot_nn(ds_ref[b], rq_ref[b])
            dv_acc[...] += dot_nn(p_ref[b], og_v[:, head_columns(h)])
            dq = dot_nn(kt[...], ds_ref[b]).T * inv_root
            dq = dq * cos_ref[...] - pltpu.roll(dq, HD // 2, 1) * sin_ref[...]
            dq_v[:, head_columns(h)] = dq.astype(BF16)

        def two_heads(i, carry):
            for b in range(2):
                products(2 * i + b, b)
            for b in range(2):
                softmax(b)
            for b in range(2):
                gradients(2 * i + b, b)
            return carry

        lax.fori_loop(0, GROUP // 2, two_heads, 0)

        kg_own[g] = dk_acc[0:LOC, :] * inv_root
        dv_own[g] = dv_acc[0:LOC, :]
        for k in range(1, BACK + 1):
            rows = slice(k * LOC, (k + 1) * LOC)
            term_send[g, 0, k - 1] = (dk_acc[rows, :] * inv_root).astype(BF16)
            term_send[g, 1, k - 1] = dv_acc[rows, :].astype(BF16)
        for kind in range(2):
            for k in range(1, BACK + 1):
                @pl.when(c >= k)
                def _(k=k, g=g, kind=kind):
                    term_copy(g, kind, k).start()

    dq_copy = pltpu.make_async_copy(dq_v, dq_hbm, local_sem.at[7])
    dq_copy.start()
    sent.append(dq_copy.wait)

    def kg_copy(s, way, g):
        zb = lax.rem(z + (NZ - s if way == 0 else s), NZ)
        part = kgt.at[zb, pl.ds(g * HD, HD), :]
        return remote(
            part, part, kg_send_sem.at[way, s, g], kg_recv_sem.at[way, s, g],
            z_peer(1 if way == 0 else NZ - 1),
        )

    kg_ring = [(s, way, g) for s in range(4) for g in range(KVH) for way in range(2) if s < 3 or g == way]
    for g in range(KVH):
        for k in range(1, BACK + 1):
            @pl.when(c + k < NCTX)
            def _(k=k, g=g):
                term_copy(g, 0, k).wait_recv()
                kg_own[g] = kg_own[g] + term_recv[g, 0, k - 1].astype(F32)
        kg = kg_own[g]
        kg = kg * cosv - pltpu.roll(kg, HD // 2, 1) * sinv
        kgt[z, pl.ds(g * HD, HD), :] = kg.T.astype(BF16)
        for way in range(2):
            kg_copy(0, way, g).start()

    def xf_copy(k):
        rows = pl.ds(pl.multiple_of(lax.rem(z + NZ - k, NZ) * LOC, LOC), LOC)
        part = xr.at[t, :, rows, :]
        return remote(part, part, xf_send_sem.at[k], xf_recv_sem.at[k], (c, d, 1 - t))

    def x_forward(k):
        if k == 0:
            for copy in x_own:
                copy.wait()
        else:
            x_copy(k, 0).wait_recv()
            x_copy(k, 1).wait_recv()
        xf_copy(k).start()

    for g in range(KVH):
        for k in range(1, BACK + 1):
            @pl.when(c + k < NCTX)
            def _(k=k, g=g):
                term_copy(g, 1, k).wait_recv()
                dv_own[g] = dv_own[g] + term_recv[g, 1, k - 1].astype(F32)
        dv_out[:, g * HD:(g + 1) * HD] = dv_own[g].astype(BF16)

    for s, way, g in kg_ring:
        kg_copy(s, way, g).wait_recv()
        if (s + 1, way, g) in kg_ring:
            kg_copy(s + 1, way, g).start()
    sources = (0, 1, 7, 2, 6, 3, 5, 4)
    x_forward(sources[0])
    sent.extend(kg_copy(s, way, g).wait_send for s, way, g in kg_ring)
    sent.append(lambda: over(0, NZ, lambda k: xf_copy(k).wait_send()))

    for n, k in enumerate(sources):
        if n + 1 < NZ:
            x_forward(sources[n + 1])
        xf_copy(k).wait_recv()
        source = lax.rem(z + NZ - k, NZ)
        tokens = pl.ds(pl.multiple_of(source * LOC, LOC), LOC)
        for i in range(2):
            for h in range(2):
                rows = slice(h * LOC, (h + 1) * LOC)
                term = dot_nn(kgt[source], xr[h, i, tokens, :])
                if n > 0:
                    term = term + gacc[i, :, rows]
                if n + 1 < NZ:
                    gacc[i, :, rows] = term
                else:
                    gtb[i, :, rows] = term.astype(BF16)

    part_rows = LOC // NCTX

    def rs_copy(k):
        p, device = plane_peer(k)
        return remote(
            gtb.at[p // NCTX, pl.ds(pl.multiple_of(lax.rem(p, NCTX) * part_rows, part_rows), part_rows), :],
            rbuf.at[k], rs_send_sem.at[k], rs_recv_sem.at[k], device,
        )

    def rs_start(k, carry):
        rs_copy(k).start()
        return carry

    lax.fori_loop(1, NPLANE, rs_start, 0)

    def rs_sum(k, total):
        rs_copy(k).wait_recv()
        return total + rbuf[k].astype(F32)

    sent.append(lambda: over(1, NPLANE, lambda k: rs_copy(k).wait_send()))
    own_rows = pl.ds(pl.multiple_of(c * part_rows, part_rows), part_rows)
    total = lax.fori_loop(1, NPLANE, rs_sum, gtb[xl, own_rows, :].astype(F32))
    gall[own_rows, :] = (total * (1.0 / math.sqrt(NDP * NCTX * LOC))).astype(BF16)

    def ga_copy(k):
        return remote(gall.at[own_rows, :], gall.at[own_rows, :], ga_send_sem.at[k], ga_recv_sem.at[k], ctx_peer(k))

    def ga_start(k, carry):
        ga_copy(k).start()
        return carry

    def ga_wait(k, carry):
        ga_copy(k).wait_recv()
        return carry

    lax.fori_loop(1, NCTX, ga_start, 0)
    for copy in opt_copies:
        copy.wait()
    lax.fori_loop(1, NCTX, ga_wait, 0)

    sent.append(lambda: over(1, NCTX, lambda k: ga_copy(k).wait_send()))
    for h in range(2):
        grad = gall[:, h * LOC:(h + 1) * LOC].astype(F32).T
        grad_out[h] = grad
        nms = adam(grad, opt_v[0, h], opt_v[1, h], opt_v[2, h])[0]
        wb[h] = nms.astype(BF16).reshape(NCTX, part_rows, LOC)

    keeps = [
        pltpu.make_async_copy(wb.at[0], kw_hbm.at[0, d], local_sem.at[8]),
        pltpu.make_async_copy(wb.at[1, c], kw_hbm.at[1, d, c], local_sem.at[9]),
    ]
    for keep in keeps:
        keep.start()

    def zs_copy(k):
        return remote(
            wb.at[1, c], kw_hbm.at[1, d, c], zs_send_sem.at[k], zs_recv_sem.at[k], z_peer(k),
        )

    swap = remote(wb.at[0], kw_hbm.at[0, d], sw_send_sem, sw_recv_sem, (c, (1 - xl) * NZ + z, t))

    def ring_copy(s, way, same, src=None):
        step = 1 if way == 0 else NZ - 1
        zb = lax.rem(z + (NZ - s if way == 0 else s), NZ)
        block = (xl if same else 1 - xl) * NZ + zb
        return remote(
            kw_hbm.at[0, block] if src is None else src, kw_hbm.at[0, block],
            ring_send_sem.at[way, s, int(same)], ring_recv_sem.at[way, s, int(same)], z_peer(step),
        )

    def zs_start(k, carry):
        zs_copy(k).start()
        return carry

    sent.append(swap.wait_send)
    sent.append(lambda: over(1, NZ, lambda k: zs_copy(k).wait_send()))
    swap.start()
    ring_copy(0, 0, True, wb.at[0]).start()
    ring_copy(0, 1, True, wb.at[0]).start()
    lax.fori_loop(1, NZ, zs_start, 0)

    def zs_wait(k, carry):
        zs_copy(k).wait_recv()
        return carry

    swap.wait_recv()
    ring_copy(0, 0, False).start()
    ring_copy(0, 1, False).start()
    lax.fori_loop(1, NZ, zs_wait, 0)
    for keep in keeps:
        keep.wait()

    def pl_copy(k):
        device = plane_peer(k)[1]
        part = kw_hbm.at[1, pl.ds(xl * NZ, NZ), c]
        return remote(part, part, pl_send_sem.at[k], pl_recv_sem.at[k], device)

    def pl_start(k, carry):
        pl_copy(k).start()
        return carry

    lax.fori_loop(1, NPLANE, pl_start, 0)

    sent.append(lambda: over(1, NPLANE, lambda k: pl_copy(k).wait_send()))
    ring = [(s, way, same) for s in range(4) for same in (True, False) for way in range(2) if s < 3 or same == (way == 0)]
    for s, way, same in ring:
        ring_copy(s, way, same).wait_recv()
        if (s + 1, way, same) in ring:
            ring_copy(s + 1, way, same).start()

    sent.extend(ring_copy(s, way, same).wait_send for s, way, same in ring)

    def pl_wait(k, carry):
        pl_copy(k).wait_recv()
        return carry

    lax.fori_loop(1, NPLANE, pl_wait, 0)

    for wait in sent:
        wait()


def on_device(
    layer_input, queries, keys, values, out_grad, doc_ids, freq_bins, master, moment1, moment2
):
    positions = lax.axis_index("ctx") * LOC + jnp.arange(LOC, dtype=jnp.int32)
    angles = positions.astype(F32)[:, None] * frequencies(freq_bins)[None, :]
    cosine = jnp.cos(angles) * magnitude_scale
    sine = jnp.sin(angles) * magnitude_scale
    cosine = jnp.concatenate([cosine, cosine], axis=1)
    sine = jnp.concatenate([-sine, sine], axis=1)

    any_ = pl.BlockSpec(memory_space=pl.ANY)
    vmem = pl.BlockSpec(memory_space=pltpu.VMEM)
    dma = pltpu.SemaphoreType.DMA
    part_rows = LOC // NCTX
    rows, cols = 2, LOC
    dq, dv, grad, kw = pl.pallas_call(
        kernel,
        out_shape=(
            jax.ShapeDtypeStruct((LOC, KVH * GROUP * HD), BF16),
            jax.ShapeDtypeStruct((LOC, KVH * HD), BF16),
            jax.ShapeDtypeStruct((rows, LOC, cols), F32),
            jax.ShapeDtypeStruct((2, NDP, NCTX, part_rows, cols), BF16),
        ),
        in_specs=[any_, any_, vmem, vmem, vmem, vmem, vmem, any_, any_, any_, any_],
        out_specs=(any_, vmem, vmem, any_),
        scratch_shapes=[
            pltpu.VMEM((LOC, KVH * GROUP * HD), BF16),
            pltpu.VMEM((LOC, KVH * GROUP * HD), BF16),
            pltpu.VMEM((LOC, KVH * GROUP * HD), BF16),
            pltpu.VMEM((KVH, 2, WIN, HD), BF16),
            pltpu.VMEM((HD, WIN), BF16),
            pltpu.VMEM((BACK + 1, 8, LOC), jnp.int32),
            pltpu.VMEM((WIN, LOC), F32),
            pltpu.VMEM((2, LOC, HD), BF16),
            pltpu.VMEM((2, WIN, LOC), F32),
            pltpu.VMEM((2, WIN, LOC), F32),
            pltpu.VMEM((2, WIN, LOC), BF16),
            pltpu.VMEM((2, WIN, LOC), BF16),
            pltpu.VMEM((WIN, HD), F32),
            pltpu.VMEM((WIN, HD), F32),
            pltpu.VMEM((KVH, 2, BACK, LOC, HD), BF16),
            pltpu.VMEM((KVH, 2, BACK, LOC, HD), BF16),
            pltpu.VMEM((KVH, LOC, HD), F32),
            pltpu.VMEM((KVH, LOC, HD), F32),
            pltpu.VMEM((2, 2, NZ * LOC, LOC), BF16),
            pltpu.VMEM((NZ, LOC, LOC), BF16),
            pltpu.VMEM((2, LOC, 2 * LOC), F32),
            pltpu.VMEM((2, LOC, 2 * LOC), BF16),
            pltpu.VMEM((NPLANE, part_rows, 2 * LOC), BF16),
            pltpu.VMEM((LOC, 2 * LOC), BF16),
            pltpu.VMEM((3, 2, LOC, LOC), F32),
            pltpu.VMEM((2, NCTX, part_rows, LOC), BF16),
            dma((10,)),
            dma((BACK,)), dma((BACK,)),
            dma((KVH, BACK)), dma((KVH, BACK)),
            dma((NZ, 2)), dma((NZ, 2)),
            dma((NZ,)), dma((NZ,)),
            dma((KVH, 2, BACK)), dma((KVH, 2, BACK)),
            dma((2, 4, KVH)), dma((2, 4, KVH)),
            dma((NPLANE,)), dma((NPLANE,)),
            dma((NCTX,)), dma((NCTX,)),
            dma, dma,
            dma((2, 4, 2)), dma((2, 4, 2)),
            dma((NZ,)), dma((NZ,)),
            dma((NPLANE,)), dma((NPLANE,)),
        ],
        compiler_params=pltpu.CompilerParams(
            collective_id=0, has_side_effects=True, vmem_limit_bytes=54 * 1024 * 1024
        ),
    )(
        queries[0], out_grad[0], keys[0], values[0], doc_ids, cosine, sine, layer_input[0],
        master, moment1, moment2,
    )
    new_master, new_moment1, new_moment2 = adam(grad, master, moment1, moment2)
    return (dq[None], dv[None], new_master, new_moment1, new_moment2, kw.reshape(2, NDP * LOC, cols))


def solution(mesh):
    placed = (
        P("dp", "ctx", "tp"),
        P("dp", "ctx", "tp"),
        P("dp", "ctx", "tp"),
        P("dp", "ctx", "tp"),
        P("dp", "ctx", "tp"),
        P("dp", "ctx"),
        P(),
        P(None, "dp", "tp"),
        P(None, "dp", "tp"),
        P(None, "dp", "tp"),
    )
    return jax.shard_map(
        on_device,
        mesh=mesh,
        in_specs=placed,
        out_specs=(
            P("dp", "ctx", "tp"),
            P("dp", "ctx", "tp"),
            P(None, "dp", "tp"),
            P(None, "dp", "tp"),
            P(None, "dp", "tp"),
            P(None, None, "tp"),
        ),
        check_vma=False,
    )
```

```python
import functools
import math

import jax
import jax.numpy as jnp
from jax import lax
from jax.experimental import pallas as pl
from jax.experimental.pallas import tpu as pltpu
from jax.sharding import PartitionSpec as P

HD = 128
BINS = 32
ADAM_STEP = 10
NCTX = 8
NDP = 16
NZ = 8
NPLANE = 16
BACK = 4
LOC = 256
GROUP = 8
KVH = 2
WIN = (BACK + 1) * LOC
CH = 128

rope_base = 10000.0
yarn_factor = 8.0
magnitude_scale = 0.1 * math.log(8.0) + 1.0
beta_first = 0.9
beta_second = 0.95
adam_epsilon = 1e-08
learn_rate = 0.0003
weight_decay = 0.1
inv_root = 1.0 / math.sqrt(HD)
MESH = pl.DeviceIdType.MESH
F32 = jnp.float32
BF16 = jnp.bfloat16


def frequencies(freq_bins):
    pairs = jnp.arange(HD // 2).astype(jnp.float32)
    theta = jnp.exp(pairs * (-2.0 * math.log(rope_base) / HD))
    gamma = freq_bins.astype(jnp.float32) / BINS
    return theta * ((1.0 - gamma) / yarn_factor + gamma)


def dot_nt(a, b):
    return lax.dot_general(a, b, (((1,), (1,)), ((), ())), preferred_element_type=F32)


def dot_nn(a, b):
    return lax.dot_general(a, b, (((1,), (0,)), ((), ())), preferred_element_type=F32)


def adam(grad, master, moment1, moment2):
    new_moment1 = beta_first * moment1 + (1.0 - beta_first) * grad
    new_moment2 = beta_second * moment2 + (1.0 - beta_second) * grad * grad
    first_fix = 1.0 - beta_first**ADAM_STEP
    second_fix = 1.0 - beta_second**ADAM_STEP
    update = new_moment1 / first_fix / (jnp.sqrt(new_moment2 / second_fix) + adam_epsilon)
    return master - learn_rate * (update + weight_decay * master), new_moment1, new_moment2


def rows8(op, value):
    return op(value.reshape(value.shape[0] // 8, 8, value.shape[1]), axis=0)


def kernel(
    q_hbm, og_hbm, k_ref, v_ref, doc_ref, cos_ref, sin_ref, x_hbm, ms_hbm, m1_hbm, m2_hbm,
    dq_hbm, dv_out, grad_out, kw_hbm,
    q_v, og_v, dq_v, kv, kt, docs, bias, rq_ref, t_ref, dp_ref, p_ref, ds_ref, dk_acc, dv_acc,
    term_send, term_recv, kg_own, dv_own, xr, kgt, gacc, gtb, rbuf, gall, opt_v, wb,
    local_sem, doc_send_sem, doc_recv_sem, kv_send_sem, kv_recv_sem, x_send_sem, x_recv_sem,
    xf_send_sem, xf_recv_sem, term_send_sem, term_recv_sem, kg_send_sem, kg_recv_sem,
    rs_send_sem, rs_recv_sem, ga_send_sem, ga_recv_sem,
    sw_send_sem, sw_recv_sem, ring_send_sem, ring_recv_sem,
    zs_send_sem, zs_recv_sem, s1_send_sem, s1_recv_sem, s2_send_sem, s2_recv_sem,
):
    c = lax.axis_index("ctx")
    d = lax.axis_index("dp")
    t = lax.axis_index("tp")
    z = lax.rem(d, NZ)
    xl = d // NZ
    me_p = xl * NCTX + c

    def z_peer(k):
        return (c, xl * NZ + lax.rem(z + k, NZ), t)

    def plane_peer(k):
        p = lax.rem(me_p + k, NPLANE)
        return p, (lax.rem(p, NCTX), (p // NCTX) * NZ + z, t)

    def ctx_peer(k):
        return (lax.rem(c + k, NCTX), d, t)

    def remote(src, dst, ssem, rsem, device):
        return pltpu.make_async_remote_copy(
            src_ref=src, dst_ref=dst, send_sem=ssem, recv_sem=rsem,
            device_id=device, device_id_type=MESH,
        )

    sent = []

    def over(low, high, one):
        def step(k, carry):
            one(k)
            return carry

        lax.fori_loop(low, high, step, 0)

    q_copy = pltpu.make_async_copy(q_hbm, q_v, local_sem.at[0])
    og_copy = pltpu.make_async_copy(og_hbm, og_v, local_sem.at[1])
    opt_copies = [
        pltpu.make_async_copy(src, opt_v.at[i], local_sem.at[2 + i])
        for i, src in enumerate((ms_hbm, m1_hbm, m2_hbm))
    ]
    x_own = [
        pltpu.make_async_copy(
            x_hbm.at[:, pl.ds(pl.multiple_of((i * NZ + z) * LOC, LOC), LOC)],
            xr.at[t, i, pl.ds(pl.multiple_of(z * LOC, LOC), LOC), :],
            local_sem.at[5 + i],
        )
        for i in range(2)
    ]
    for copy in [q_copy, og_copy] + opt_copies + x_own:
        copy.start()

    barrier = pltpu.get_barrier_semaphore()

    def greet_z(k, carry):
        pl.semaphore_signal(barrier, inc=1, device_id=z_peer(k), device_id_type=MESH)
        return carry

    def greet_plane(k, carry):
        pl.semaphore_signal(barrier, inc=1, device_id=plane_peer(k)[1], device_id_type=MESH)
        return carry

    lax.fori_loop(1, NZ, greet_z, 0)
    lax.fori_loop(1, NPLANE, greet_plane, 0)
    pl.semaphore_signal(barrier, inc=1, device_id=(c, d, 1 - t), device_id_type=MESH)

    cosv = cos_ref[...]
    sinv = sin_ref[...]
    for g in range(KVH):
        kh = k_ref[:, g * HD:(g + 1) * HD].astype(F32)
        kv[g, 0, 0:LOC, :] = (kh * cosv + pltpu.roll(kh, HD // 2, 1) * sinv).astype(BF16)
        kv[g, 1, 0:LOC, :] = v_ref[:, g * HD:(g + 1) * HD]
    docs[0] = jnp.broadcast_to(doc_ref[...], (8, LOC))

    pl.semaphore_wait(barrier, (NZ - 1) + (NPLANE - 1) + 1)

    def doc_copy(k):
        return remote(docs.at[0], docs.at[k], doc_send_sem.at[k - 1], doc_recv_sem.at[k - 1], ctx_peer(k))

    def kv_copy(g, k):
        return remote(
            kv.at[g, :, pl.ds(0, LOC), :], kv.at[g, :, pl.ds(k * LOC, LOC), :],
            kv_send_sem.at[g, k - 1], kv_recv_sem.at[g, k - 1], ctx_peer(k),
        )

    for k in range(BACK, 0, -1):
        @pl.when(c + k < NCTX)
        def _(k=k):
            doc_copy(k).start()
            kv_copy(0, k).start()

    def kv_sent():
        for k in range(1, BACK + 1):
            @pl.when(c + k < NCTX)
            def _(k=k):
                doc_copy(k).wait_send()
                for g in range(KVH):
                    kv_copy(g, k).wait_send()

    sent.append(kv_sent)

    def x_copy(k, i):
        zd = lax.rem(z + k, NZ)
        return remote(
            x_hbm.at[:, pl.ds(pl.multiple_of((i * NZ + zd) * LOC, LOC), LOC)],
            xr.at[t, i, pl.ds(pl.multiple_of(z * LOC, LOC), LOC), :],
            x_send_sem.at[k, i], x_recv_sem.at[k, i], z_peer(k),
        )

    def x_start(k, carry):
        x_copy(k, 0).start()
        x_copy(k, 1).start()
        return carry

    def x_sent(k):
        x_copy(k, 0).wait_send()
        x_copy(k, 1).wait_send()

    sent.append(lambda: over(1, NZ, x_sent))

    lax.fori_loop(1, NZ, x_start, 0)

    for k in range(1, BACK + 1):
        @pl.when(c + k < NCTX)
        def _(k=k):
            kv_copy(1, k).start()

        @pl.when(c < k)
        def _(k=k):
            kv[:, :, k * LOC:(k + 1) * LOC, :] = jnp.zeros((KVH, 2, LOC, HD), BF16)
            docs[k] = jnp.full((8, LOC), 127, jnp.int32)

    for k in range(1, BACK + 1):
        @pl.when(c >= k)
        def _(k=k):
            doc_copy(k).wait_recv()
    own_docs = doc_ref[...]
    window_start = jnp.maximum(c - BACK, 0) * LOC
    start = jnp.zeros((1, LOC), F32)
    for doc in range(1, 4):
        below = jnp.zeros((8, LOC), F32)
        for k in range(BACK + 1):
            below = below + (docs[k] < doc).astype(F32)
        count = jnp.sum(below[0:1], axis=1, keepdims=True)
        start = jnp.where(own_docs == doc, count, start)
    start = start.astype(jnp.int32) + window_start
    query_pos = c * LOC + lax.broadcasted_iota(jnp.int32, (1, LOC), 1)
    for k in range(BACK + 1):
        key_pos = (c - k) * LOC + lax.broadcasted_iota(jnp.int32, (LOC, LOC), 0)
        seen = (key_pos <= query_pos) & (key_pos >= start)
        bias[k * LOC:(k + 1) * LOC, :] = jnp.where(seen, 0.0, -jnp.inf)

    q_copy.wait()
    og_copy.wait()
    scale2 = inv_root * math.log2(math.e)
    chunks = [slice(j * CH, (j + 1) * CH) for j in range(WIN // CH)]

    def term_copy(g, kind, k):
        return remote(
            term_send.at[g, kind, k - 1], term_recv.at[g, kind, k - 1],
            term_send_sem.at[g, kind, k - 1], term_recv_sem.at[g, kind, k - 1],
            ctx_peer(NCTX - k),
        )

    def term_sent(g):
        for k in range(1, BACK + 1):
            @pl.when(c >= k)
            def _(k=k):
                for kind in range(2):
                    term_copy(g, kind, k).wait_send()

    sent.append(lambda: term_sent(0))
    sent.append(lambda: term_sent(1))
    for g in range(KVH):
        for k in range(1, BACK + 1):
            @pl.when(c >= k)
            def _(k=k, g=g):
                kv_copy(g, k).wait_recv()
        for sl in chunks:
            kt[:, sl] = kv[g, 0, sl, :].astype(F32).T.astype(BF16)
        dk_acc[...] = jnp.zeros_like(dk_acc)
        dv_acc[...] = jnp.zeros_like(dv_acc)

        def head_columns(h, g=g):
            return pl.ds(pl.multiple_of((g * GROUP + h) * HD, HD), HD)

        def products(h, b, g=g):
            qh = q_v[:, head_columns(h)].astype(F32)
            rq = (qh * cos_ref[...] + pltpu.roll(qh, HD // 2, 1) * sin_ref[...]).astype(BF16)
            rq_ref[b] = rq
            t_ref[b] = dot_nt(kv[g, 0], rq)
            dp_ref[b] = dot_nt(kv[g, 1], og_v[:, head_columns(h)])

        def softmax(b):
            top = None
            for sl in chunks:
                score = t_ref[b, sl, :] * scale2 + bias[sl, :]
                t_ref[b, sl, :] = score
                part = rows8(jnp.max, score)
                top = part if top is None else jnp.maximum(top, part)
            top = jnp.max(top, axis=0, keepdims=True)
            total = jnp.zeros((8, LOC), F32)
            mixed = jnp.zeros((8, LOC), F32)
            for sl in chunks:
                e = jnp.exp2(t_ref[b, sl, :] - top)
                t_ref[b, sl, :] = e
                total = total + rows8(jnp.sum, e)
                mixed = mixed + rows8(jnp.sum, e * dp_ref[b, sl, :])
            inv_total = 1.0 / jnp.sum(total, axis=0, keepdims=True)
            delta = jnp.sum(mixed, axis=0, keepdims=True) * inv_total
            for sl in chunks:
                p = t_ref[b, sl, :] * inv_total
                ds_ref[b, sl, :] = (p * (dp_ref[b, sl, :] - delta)).astype(BF16)
                p_ref[b, sl, :] = p.astype(BF16)

        def gradients(h, b):
            dk_acc[...] += dot_nn(ds_ref[b], rq_ref[b])
            dv_acc[...] += dot_nn(p_ref[b], og_v[:, head_columns(h)])
            dq = dot_nn(kt[...], ds_ref[b]).T * inv_root
            dq = dq * cos_ref[...] - pltpu.roll(dq, HD // 2, 1) * sin_ref[...]
            dq_v[:, head_columns(h)] = dq.astype(BF16)

        def two_heads(i, carry):
            for b in range(2):
                products(2 * i + b, b)
            for b in range(2):
                softmax(b)
            for b in range(2):
                gradients(2 * i + b, b)
            return carry

        lax.fori_loop(0, GROUP // 2, two_heads, 0)

        kg_own[g] = dk_acc[0:LOC, :] * inv_root
        dv_own[g] = dv_acc[0:LOC, :]
        for k in range(1, BACK + 1):
            rows = slice(k * LOC, (k + 1) * LOC)
            term_send[g, 0, k - 1] = (dk_acc[rows, :] * inv_root).astype(BF16)
            term_send[g, 1, k - 1] = dv_acc[rows, :].astype(BF16)
        for kind in range(2):
            for k in range(BACK, 0, -1):
                @pl.when(c >= k)
                def _(k=k, g=g, kind=kind):
                    term_copy(g, kind, k).start()

    dq_copy = pltpu.make_async_copy(dq_v, dq_hbm, local_sem.at[7])
    dq_copy.start()
    sent.append(dq_copy.wait)

    def kg_copy(s, way, g):
        zb = lax.rem(z + (NZ - s if way == 0 else s), NZ)
        part = kgt.at[zb, pl.ds(g * HD, HD), :]
        return remote(
            part, part, kg_send_sem.at[way, s, g], kg_recv_sem.at[way, s, g],
            z_peer(1 if way == 0 else NZ - 1),
        )

    kg_ring = [(s, way, g) for s in range(4) for g in range(KVH) for way in range(2) if s < 3 or g == way]
    for g in range(KVH):
        for k in range(1, BACK + 1):
            @pl.when(c + k < NCTX)
            def _(k=k, g=g):
                term_copy(g, 0, k).wait_recv()
                kg_own[g] = kg_own[g] + term_recv[g, 0, k - 1].astype(F32)
        kg = kg_own[g]
        kg = kg * cosv - pltpu.roll(kg, HD // 2, 1) * sinv
        kgt[z, pl.ds(g * HD, HD), :] = kg.T.astype(BF16)
        for way in range(2):
            kg_copy(0, way, g).start()

    def xf_copy(k):
        rows = pl.ds(pl.multiple_of(lax.rem(z + NZ - k, NZ) * LOC, LOC), LOC)
        part = xr.at[t, :, rows, :]
        return remote(part, part, xf_send_sem.at[k], xf_recv_sem.at[k], (c, d, 1 - t))

    def x_forward(k):
        if k == 0:
            for copy in x_own:
                copy.wait()
        else:
            x_copy(k, 0).wait_recv()
            x_copy(k, 1).wait_recv()
        xf_copy(k).start()

    for g in range(KVH):
        for k in range(1, BACK + 1):
            @pl.when(c + k < NCTX)
            def _(k=k, g=g):
                term_copy(g, 1, k).wait_recv()
                dv_own[g] = dv_own[g] + term_recv[g, 1, k - 1].astype(F32)
        dv_out[:, g * HD:(g + 1) * HD] = dv_own[g].astype(BF16)

    for s, way, g in kg_ring:
        kg_copy(s, way, g).wait_recv()
        if (s + 1, way, g) in kg_ring:
            kg_copy(s + 1, way, g).start()
    sources = (0, 1, 7, 2, 6, 3, 5, 4)
    x_forward(sources[0])
    sent.extend(kg_copy(s, way, g).wait_send for s, way, g in kg_ring)
    sent.append(lambda: over(0, NZ, lambda k: xf_copy(k).wait_send()))

    for n, k in enumerate(sources):
        if n + 1 < NZ:
            x_forward(sources[n + 1])
        xf_copy(k).wait_recv()
        source = lax.rem(z + NZ - k, NZ)
        tokens = pl.ds(pl.multiple_of(source * LOC, LOC), LOC)
        for i in range(2):
            for h in range(2):
                rows = slice(h * LOC, (h + 1) * LOC)
                term = dot_nn(kgt[source], xr[h, i, tokens, :])
                if n > 0:
                    term = term + gacc[i, :, rows]
                if n + 1 < NZ:
                    gacc[i, :, rows] = term
                else:
                    gtb[i, :, rows] = term.astype(BF16)

    part_rows = LOC // NCTX

    def rs_copy(k):
        p, device = plane_peer(k)
        return remote(
            gtb.at[p // NCTX, pl.ds(pl.multiple_of(lax.rem(p, NCTX) * part_rows, part_rows), part_rows), :],
            rbuf.at[k], rs_send_sem.at[k], rs_recv_sem.at[k], device,
        )

    def rs_start(k, carry):
        rs_copy(k).start()
        return carry

    lax.fori_loop(1, NPLANE, rs_start, 0)

    def rs_sum(k, total):
        rs_copy(k).wait_recv()
        return total + rbuf[k].astype(F32)

    sent.append(lambda: over(1, NPLANE, lambda k: rs_copy(k).wait_send()))
    own_rows = pl.ds(pl.multiple_of(c * part_rows, part_rows), part_rows)
    total = lax.fori_loop(1, NPLANE, rs_sum, gtb[xl, own_rows, :].astype(F32))
    gall[own_rows, :] = (total * (1.0 / math.sqrt(NDP * NCTX * LOC))).astype(BF16)

    def ga_copy(k):
        return remote(gall.at[own_rows, :], gall.at[own_rows, :], ga_send_sem.at[k], ga_recv_sem.at[k], ctx_peer(k))

    def ga_start(k, carry):
        ga_copy(k).start()
        return carry

    def ga_wait(k, carry):
        ga_copy(k).wait_recv()
        return carry

    lax.fori_loop(1, NCTX, ga_start, 0)
    for copy in opt_copies:
        copy.wait()
    lax.fori_loop(1, NCTX, ga_wait, 0)

    sent.append(lambda: over(1, NCTX, lambda k: ga_copy(k).wait_send()))
    for h in range(2):
        grad = gall[:, h * LOC:(h + 1) * LOC].astype(F32).T
        grad_out[h] = grad
        nms = adam(grad, opt_v[0, h], opt_v[1, h], opt_v[2, h])[0]
        wb[h] = nms.astype(BF16).reshape(NCTX, part_rows, LOC)

    keeps = [
        pltpu.make_async_copy(wb.at[0], kw_hbm.at[0, d], local_sem.at[8]),
        pltpu.make_async_copy(wb.at[1, c], kw_hbm.at[1, d, c], local_sem.at[9]),
    ]
    for keep in keeps:
        keep.start()

    def zs_copy(k):
        return remote(
            wb.at[1, c], kw_hbm.at[1, d, c], zs_send_sem.at[k], zs_recv_sem.at[k], z_peer(k),
        )

    swap = remote(wb.at[0], kw_hbm.at[0, d], sw_send_sem, sw_recv_sem, (c, (1 - xl) * NZ + z, t))

    def ring_copy(s, way, same, src=None):
        step = 1 if way == 0 else NZ - 1
        zb = lax.rem(z + (NZ - s if way == 0 else s), NZ)
        block = (xl if same else 1 - xl) * NZ + zb
        return remote(
            kw_hbm.at[0, block] if src is None else src, kw_hbm.at[0, block],
            ring_send_sem.at[way, s, int(same)], ring_recv_sem.at[way, s, int(same)], z_peer(step),
        )

    over(1, NZ, lambda k: zs_copy(k).start())
    swap.start()
    ring_copy(0, 0, True, wb.at[0]).start()
    ring_copy(0, 1, True, wb.at[0]).start()
    swap.wait_recv()
    ring_copy(0, 0, False).start()
    ring_copy(0, 1, False).start()
    over(1, NZ, lambda k: zs_copy(k).wait_recv())
    for keep in keeps:
        keep.wait()

    y = c // 2
    x = 2 * lax.rem(c, 2) + xl

    def chip(xx, yy):
        xx, yy = lax.rem(xx, 4), lax.rem(yy, 4)
        return (2 * yy + xx // 2, lax.rem(xx, 2) * NZ + z, t)

    def piece(xx, yy, first):
        xx, yy = lax.rem(xx, 4), lax.rem(yy, 4)
        return kw_hbm.at[1, pl.ds(lax.rem(xx, 2) * NZ + first * (NZ // 2), NZ // 2), 2 * yy + xx // 2]

    def stage1(first, j):
        part = piece(x, y, first)
        device = chip(x + j, y) if first == 0 else chip(x, y + j)
        return remote(part, part, s1_send_sem.at[first, j], s1_recv_sem.at[first, j], device)

    def stage2(first, a, j):
        part = piece(x + 4 - a, y, first) if first == 0 else piece(x, y + 4 - a, first)
        device = chip(x, y + j) if first == 0 else chip(x + j, y)
        return remote(part, part, s2_send_sem.at[first, a, j], s2_recv_sem.at[first, a, j], device)

    ring = [(s, way, same) for s in range(4) for same in (True, False) for way in range(2) if s < 3 or same == (way == 0)]

    def ring_step(step):
        for s, way, same in ring:
            if s == step:
                ring_copy(s, way, same).wait_recv()
                if (s + 1, way, same) in ring:
                    ring_copy(s + 1, way, same).start()

    for j in (2, 1, 3):
        for first in range(2):
            stage1(first, j).start()
    for j in (2, 1, 3):
        for first in range(2):
            stage2(first, 0, j).start()
    ring_step(0)
    for step, a in enumerate((1, 3, 2)):
        for first in range(2):
            stage1(first, a).wait_recv()
            over(1, 4, lambda j: stage2(first, a, j).start())
        ring_step(step + 1)
    for first in range(2):
        for a in range(4):
            over(1, 4, lambda j: stage2(first, a, j).wait_recv())

    sent.append(swap.wait_send)
    sent.append(lambda: over(1, NZ, lambda k: zs_copy(k).wait_send()))
    sent.extend(ring_copy(s, way, same).wait_send for s, way, same in ring)
    for first in range(2):
        sent.append(lambda first=first: over(1, 4, lambda j: stage1(first, j).wait_send()))
        for a in range(4):
            sent.append(lambda first=first, a=a: over(1, 4, lambda j: stage2(first, a, j).wait_send()))

    for wait in sent:
        wait()


def on_device(
    layer_input, queries, keys, values, out_grad, doc_ids, freq_bins, master, moment1, moment2
):
    positions = lax.axis_index("ctx") * LOC + jnp.arange(LOC, dtype=jnp.int32)
    angles = positions.astype(F32)[:, None] * frequencies(freq_bins)[None, :]
    cosine = jnp.cos(angles) * magnitude_scale
    sine = jnp.sin(angles) * magnitude_scale
    cosine = jnp.concatenate([cosine, cosine], axis=1)
    sine = jnp.concatenate([-sine, sine], axis=1)

    any_ = pl.BlockSpec(memory_space=pl.ANY)
    vmem = pl.BlockSpec(memory_space=pltpu.VMEM)
    dma = pltpu.SemaphoreType.DMA
    part_rows = LOC // NCTX
    rows, cols = 2, LOC
    dq, dv, grad, kw = pl.pallas_call(
        kernel,
        out_shape=(
            jax.ShapeDtypeStruct((LOC, KVH * GROUP * HD), BF16),
            jax.ShapeDtypeStruct((LOC, KVH * HD), BF16),
            jax.ShapeDtypeStruct((rows, LOC, cols), F32),
            jax.ShapeDtypeStruct((2, NDP, NCTX, part_rows, cols), BF16),
        ),
        in_specs=[any_, any_, vmem, vmem, vmem, vmem, vmem, any_, any_, any_, any_],
        out_specs=(any_, vmem, vmem, any_),
        scratch_shapes=[
            pltpu.VMEM((LOC, KVH * GROUP * HD), BF16),
            pltpu.VMEM((LOC, KVH * GROUP * HD), BF16),
            pltpu.VMEM((LOC, KVH * GROUP * HD), BF16),
            pltpu.VMEM((KVH, 2, WIN, HD), BF16),
            pltpu.VMEM((HD, WIN), BF16),
            pltpu.VMEM((BACK + 1, 8, LOC), jnp.int32),
            pltpu.VMEM((WIN, LOC), F32),
            pltpu.VMEM((2, LOC, HD), BF16),
            pltpu.VMEM((2, WIN, LOC), F32),
            pltpu.VMEM((2, WIN, LOC), F32),
            pltpu.VMEM((2, WIN, LOC), BF16),
            pltpu.VMEM((2, WIN, LOC), BF16),
            pltpu.VMEM((WIN, HD), F32),
            pltpu.VMEM((WIN, HD), F32),
            pltpu.VMEM((KVH, 2, BACK, LOC, HD), BF16),
            pltpu.VMEM((KVH, 2, BACK, LOC, HD), BF16),
            pltpu.VMEM((KVH, LOC, HD), F32),
            pltpu.VMEM((KVH, LOC, HD), F32),
            pltpu.VMEM((2, 2, NZ * LOC, LOC), BF16),
            pltpu.VMEM((NZ, LOC, LOC), BF16),
            pltpu.VMEM((2, LOC, 2 * LOC), F32),
            pltpu.VMEM((2, LOC, 2 * LOC), BF16),
            pltpu.VMEM((NPLANE, part_rows, 2 * LOC), BF16),
            pltpu.VMEM((LOC, 2 * LOC), BF16),
            pltpu.VMEM((3, 2, LOC, LOC), F32),
            pltpu.VMEM((2, NCTX, part_rows, LOC), BF16),
            dma((10,)),
            dma((BACK,)), dma((BACK,)),
            dma((KVH, BACK)), dma((KVH, BACK)),
            dma((NZ, 2)), dma((NZ, 2)),
            dma((NZ,)), dma((NZ,)),
            dma((KVH, 2, BACK)), dma((KVH, 2, BACK)),
            dma((2, 4, KVH)), dma((2, 4, KVH)),
            dma((NPLANE,)), dma((NPLANE,)),
            dma((NCTX,)), dma((NCTX,)),
            dma, dma,
            dma((2, 4, 2)), dma((2, 4, 2)),
            dma((NZ,)), dma((NZ,)),
            dma((2, 4)), dma((2, 4)),
            dma((2, 4, 4)), dma((2, 4, 4)),
        ],
        compiler_params=pltpu.CompilerParams(
            collective_id=0, has_side_effects=True, vmem_limit_bytes=54 * 1024 * 1024
        ),
    )(
        queries[0], out_grad[0], keys[0], values[0], doc_ids, cosine, sine, layer_input[0],
        master, moment1, moment2,
    )
    new_master, new_moment1, new_moment2 = adam(grad, master, moment1, moment2)
    return (dq[None], dv[None], new_master, new_moment1, new_moment2, kw.reshape(2, NDP * LOC, cols))


def solution(mesh):
    placed = (
        P("dp", "ctx", "tp"),
        P("dp", "ctx", "tp"),
        P("dp", "ctx", "tp"),
        P("dp", "ctx", "tp"),
        P("dp", "ctx", "tp"),
        P("dp", "ctx"),
        P(),
        P(None, "dp", "tp"),
        P(None, "dp", "tp"),
        P(None, "dp", "tp"),
    )
    return jax.shard_map(
        on_device,
        mesh=mesh,
        in_specs=placed,
        out_specs=(
            P("dp", "ctx", "tp"),
            P("dp", "ctx", "tp"),
            P(None, "dp", "tp"),
            P(None, "dp", "tp"),
            P(None, "dp", "tp"),
            P(None, None, "tp"),
        ),
        check_vma=False,
    )
```

```python
import functools
import math

import jax
import jax.numpy as jnp
from jax import lax
from jax.experimental import pallas as pl
from jax.experimental.pallas import tpu as pltpu
from jax.sharding import PartitionSpec as P

HD = 128
BINS = 32
ADAM_STEP = 10
NCTX = 8
NDP = 16
NZ = 8
NPLANE = 16
BACK = 4
LOC = 256
GROUP = 8
KVH = 2
WIN = (BACK + 1) * LOC
CH = 128

rope_base = 10000.0
yarn_factor = 8.0
magnitude_scale = 0.1 * math.log(8.0) + 1.0
beta_first = 0.9
beta_second = 0.95
adam_epsilon = 1e-08
learn_rate = 0.0003
weight_decay = 0.1
inv_root = 1.0 / math.sqrt(HD)
MESH = pl.DeviceIdType.MESH
F32 = jnp.float32
BF16 = jnp.bfloat16


def frequencies(freq_bins):
    pairs = jnp.arange(HD // 2).astype(jnp.float32)
    theta = jnp.exp(pairs * (-2.0 * math.log(rope_base) / HD))
    gamma = freq_bins.astype(jnp.float32) / BINS
    return theta * ((1.0 - gamma) / yarn_factor + gamma)


def dot_nt(a, b):
    return lax.dot_general(a, b, (((1,), (1,)), ((), ())), preferred_element_type=F32)


def dot_nn(a, b):
    return lax.dot_general(a, b, (((1,), (0,)), ((), ())), preferred_element_type=F32)


def adam(grad, master, moment1, moment2):
    new_moment1 = beta_first * moment1 + (1.0 - beta_first) * grad
    new_moment2 = beta_second * moment2 + (1.0 - beta_second) * grad * grad
    first_fix = 1.0 - beta_first**ADAM_STEP
    second_fix = 1.0 - beta_second**ADAM_STEP
    update = new_moment1 / first_fix / (jnp.sqrt(new_moment2 / second_fix) + adam_epsilon)
    return master - learn_rate * (update + weight_decay * master), new_moment1, new_moment2


def rows8(op, value):
    return op(value.reshape(value.shape[0] // 8, 8, value.shape[1]), axis=0)


def kernel(
    q_hbm, og_hbm, k_ref, v_ref, doc_ref, cos_ref, sin_ref, x_hbm, ms_hbm, m1_hbm, m2_hbm,
    dq_hbm, dv_out, grad_out, kw_hbm,
    q_v, og_v, dq_v, kv, kt, docs, bias, rq_ref, t_ref, dp_ref, p_ref, ds_ref, dk_acc, dv_acc,
    term_send, term_recv, kg_own, dv_own, xr, kgt, gacc, gtb, rbuf, gall, opt_v, wb,
    local_sem, doc_send_sem, doc_recv_sem, kv_send_sem, kv_recv_sem, x_send_sem, x_recv_sem,
    xf_send_sem, xf_recv_sem, term_send_sem, term_recv_sem, kg_send_sem, kg_recv_sem,
    rs_send_sem, rs_recv_sem, ga_send_sem, ga_recv_sem,
    sw_send_sem, sw_recv_sem, ring_send_sem, ring_recv_sem,
    zs_send_sem, zs_recv_sem, s1_send_sem, s1_recv_sem, s2_send_sem, s2_recv_sem,
):
    c = lax.axis_index("ctx")
    d = lax.axis_index("dp")
    t = lax.axis_index("tp")
    z = lax.rem(d, NZ)
    xl = d // NZ
    me_p = xl * NCTX + c

    def z_peer(k):
        return (c, xl * NZ + lax.rem(z + k, NZ), t)

    def plane_peer(k):
        p = lax.rem(me_p + k, NPLANE)
        return p, (lax.rem(p, NCTX), (p // NCTX) * NZ + z, t)

    def ctx_peer(k):
        return (lax.rem(c + k, NCTX), d, t)

    def remote(src, dst, ssem, rsem, device):
        return pltpu.make_async_remote_copy(
            src_ref=src, dst_ref=dst, send_sem=ssem, recv_sem=rsem,
            device_id=device, device_id_type=MESH,
        )

    sent = []

    def over(low, high, one):
        def step(k, carry):
            one(k)
            return carry

        lax.fori_loop(low, high, step, 0)

    q_copy = pltpu.make_async_copy(q_hbm, q_v, local_sem.at[0])
    og_copy = pltpu.make_async_copy(og_hbm, og_v, local_sem.at[1])
    opt_copies = [
        pltpu.make_async_copy(src, opt_v.at[i], local_sem.at[2 + i])
        for i, src in enumerate((ms_hbm, m1_hbm, m2_hbm))
    ]
    x_own = [
        pltpu.make_async_copy(
            x_hbm.at[:, pl.ds(pl.multiple_of((i * NZ + z) * LOC, LOC), LOC)],
            xr.at[t, i, pl.ds(pl.multiple_of(z * LOC, LOC), LOC), :],
            local_sem.at[5 + i],
        )
        for i in range(2)
    ]
    for copy in [q_copy, og_copy] + opt_copies + x_own:
        copy.start()

    barrier = pltpu.get_barrier_semaphore()

    def greet_z(k, carry):
        pl.semaphore_signal(barrier, inc=1, device_id=z_peer(k), device_id_type=MESH)
        return carry

    def greet_plane(k, carry):
        pl.semaphore_signal(barrier, inc=1, device_id=plane_peer(k)[1], device_id_type=MESH)
        return carry

    lax.fori_loop(1, NZ, greet_z, 0)
    lax.fori_loop(1, NPLANE, greet_plane, 0)
    pl.semaphore_signal(barrier, inc=1, device_id=(c, d, 1 - t), device_id_type=MESH)

    cosv = cos_ref[...]
    sinv = sin_ref[...]
    for g in range(KVH):
        kh = k_ref[:, g * HD:(g + 1) * HD].astype(F32)
        kv[g, 0, 0:LOC, :] = (kh * cosv + pltpu.roll(kh, HD // 2, 1) * sinv).astype(BF16)
        kv[g, 1, 0:LOC, :] = v_ref[:, g * HD:(g + 1) * HD]
    docs[0] = jnp.broadcast_to(doc_ref[...], (8, LOC))

    pl.semaphore_wait(barrier, (NZ - 1) + (NPLANE - 1) + 1)

    def doc_copy(k):
        return remote(docs.at[0], docs.at[k], doc_send_sem.at[k - 1], doc_recv_sem.at[k - 1], ctx_peer(k))

    def kv_copy(g, k):
        return remote(
            kv.at[g, :, pl.ds(0, LOC), :], kv.at[g, :, pl.ds(k * LOC, LOC), :],
            kv_send_sem.at[g, k - 1], kv_recv_sem.at[g, k - 1], ctx_peer(k),
        )

    for k in range(BACK, 0, -1):
        @pl.when(c + k < NCTX)
        def _(k=k):
            doc_copy(k).start()
            kv_copy(0, k).start()

    def kv_sent():
        for k in range(1, BACK + 1):
            @pl.when(c + k < NCTX)
            def _(k=k):
                doc_copy(k).wait_send()
                for g in range(KVH):
                    kv_copy(g, k).wait_send()

    sent.append(kv_sent)

    def x_copy(k, i):
        zd = lax.rem(z + k, NZ)
        return remote(
            x_hbm.at[:, pl.ds(pl.multiple_of((i * NZ + zd) * LOC, LOC), LOC)],
            xr.at[t, i, pl.ds(pl.multiple_of(z * LOC, LOC), LOC), :],
            x_send_sem.at[k, i], x_recv_sem.at[k, i], z_peer(k),
        )

    def x_start(k, carry):
        x_copy(k, 0).start()
        x_copy(k, 1).start()
        return carry

    def x_sent(k):
        x_copy(k, 0).wait_send()
        x_copy(k, 1).wait_send()

    sent.append(lambda: over(1, NZ, x_sent))

    lax.fori_loop(1, NZ, x_start, 0)

    for k in range(1, BACK + 1):
        @pl.when(c + k < NCTX)
        def _(k=k):
            kv_copy(1, k).start()

        @pl.when(c < k)
        def _(k=k):
            kv[:, :, k * LOC:(k + 1) * LOC, :] = jnp.zeros((KVH, 2, LOC, HD), BF16)
            docs[k] = jnp.full((8, LOC), 127, jnp.int32)

    for k in range(1, BACK + 1):
        @pl.when(c >= k)
        def _(k=k):
            doc_copy(k).wait_recv()
    own_docs = doc_ref[...]
    window_start = jnp.maximum(c - BACK, 0) * LOC
    start = jnp.zeros((1, LOC), F32)
    for doc in range(1, 4):
        below = jnp.zeros((8, LOC), F32)
        for k in range(BACK + 1):
            below = below + (docs[k] < doc).astype(F32)
        count = jnp.sum(below[0:1], axis=1, keepdims=True)
        start = jnp.where(own_docs == doc, count, start)
    start = start.astype(jnp.int32) + window_start
    query_pos = c * LOC + lax.broadcasted_iota(jnp.int32, (1, LOC), 1)
    for k in range(BACK + 1):
        key_pos = (c - k) * LOC + lax.broadcasted_iota(jnp.int32, (LOC, LOC), 0)
        seen = (key_pos <= query_pos) & (key_pos >= start)
        bias[k * LOC:(k + 1) * LOC, :] = jnp.where(seen, 0.0, -jnp.inf)

    q_copy.wait()
    og_copy.wait()
    scale2 = inv_root * math.log2(math.e)
    chunks = [slice(j * CH, (j + 1) * CH) for j in range(WIN // CH)]

    def term_copy(g, kind, k):
        return remote(
            term_send.at[g, kind, k - 1], term_recv.at[g, kind, k - 1],
            term_send_sem.at[g, kind, k - 1], term_recv_sem.at[g, kind, k - 1],
            ctx_peer(NCTX - k),
        )

    def term_sent(g):
        for k in range(1, BACK + 1):
            @pl.when(c >= k)
            def _(k=k):
                for kind in range(2):
                    term_copy(g, kind, k).wait_send()

    sent.append(lambda: term_sent(0))
    sent.append(lambda: term_sent(1))
    def kg_copy(s, way, g):
        zb = lax.rem(z + (NZ - s if way == 0 else s), NZ)
        part = kgt.at[zb, pl.ds(g * HD, HD), :]
        return remote(
            part, part, kg_send_sem.at[way, s, g], kg_recv_sem.at[way, s, g],
            z_peer(1 if way == 0 else NZ - 1),
        )

    kg_ring = [(s, way, g) for s in range(4) for g in range(KVH) for way in range(2) if s < 3 or g == way]

    def key_gradient(g):
        for k in range(1, BACK + 1):
            @pl.when(c + k < NCTX)
            def _(k=k):
                term_copy(g, 0, k).wait_recv()
                kg_own[g] = kg_own[g] + term_recv[g, 0, k - 1].astype(F32)
        kg = kg_own[g]
        kg = kg * cos_ref[...] - pltpu.roll(kg, HD // 2, 1) * sin_ref[...]
        kgt[z, pl.ds(g * HD, HD), :] = kg.T.astype(BF16)
        for way in range(2):
            kg_copy(0, way, g).start()

    def kg_step(step, head):
        for s, way, g in kg_ring:
            if s == step and g == head:
                kg_copy(s, way, g).wait_recv()
                if (s + 1, way, g) in kg_ring:
                    kg_copy(s + 1, way, g).start()

    for g in range(KVH):
        for k in range(1, BACK + 1):
            @pl.when(c >= k)
            def _(k=k, g=g):
                kv_copy(g, k).wait_recv()
        for sl in chunks:
            kt[:, sl] = kv[g, 0, sl, :].astype(F32).T.astype(BF16)
        dk_acc[...] = jnp.zeros_like(dk_acc)
        dv_acc[...] = jnp.zeros_like(dv_acc)

        def head_columns(h, g=g):
            return pl.ds(pl.multiple_of((g * GROUP + h) * HD, HD), HD)

        def products(h, b, g=g):
            qh = q_v[:, head_columns(h)].astype(F32)
            rq = (qh * cos_ref[...] + pltpu.roll(qh, HD // 2, 1) * sin_ref[...]).astype(BF16)
            rq_ref[b] = rq
            t_ref[b] = dot_nt(kv[g, 0], rq)
            dp_ref[b] = dot_nt(kv[g, 1], og_v[:, head_columns(h)])

        def softmax(b):
            top = None
            for sl in chunks:
                score = t_ref[b, sl, :] * scale2 + bias[sl, :]
                t_ref[b, sl, :] = score
                part = rows8(jnp.max, score)
                top = part if top is None else jnp.maximum(top, part)
            top = jnp.max(top, axis=0, keepdims=True)
            total = jnp.zeros((8, LOC), F32)
            mixed = jnp.zeros((8, LOC), F32)
            for sl in chunks:
                e = jnp.exp2(t_ref[b, sl, :] - top)
                t_ref[b, sl, :] = e
                total = total + rows8(jnp.sum, e)
                mixed = mixed + rows8(jnp.sum, e * dp_ref[b, sl, :])
            inv_total = 1.0 / jnp.sum(total, axis=0, keepdims=True)
            delta = jnp.sum(mixed, axis=0, keepdims=True) * inv_total
            for sl in chunks:
                p = t_ref[b, sl, :] * inv_total
                ds_ref[b, sl, :] = (p * (dp_ref[b, sl, :] - delta)).astype(BF16)
                p_ref[b, sl, :] = p.astype(BF16)

        def gradients(h, b):
            dk_acc[...] += dot_nn(ds_ref[b], rq_ref[b])
            dv_acc[...] += dot_nn(p_ref[b], og_v[:, head_columns(h)])
            dq = dot_nn(kt[...], ds_ref[b]).T * inv_root
            dq = dq * cos_ref[...] - pltpu.roll(dq, HD // 2, 1) * sin_ref[...]
            dq_v[:, head_columns(h)] = dq.astype(BF16)

        def two_heads(i, carry, g=g):
            for b in range(2):
                products(2 * i + b, b)
            for b in range(2):
                softmax(b)
            for b in range(2):
                gradients(2 * i + b, b)
            if g == 1:
                pl.when(i == 1)(lambda: key_gradient(0))
                pl.when(i == 2)(lambda: kg_step(0, 0))
                pl.when(i == 3)(lambda: kg_step(1, 0))
            return carry

        lax.fori_loop(0, GROUP // 2, two_heads, 0)

        kg_own[g] = dk_acc[0:LOC, :] * inv_root
        dv_own[g] = dv_acc[0:LOC, :]
        for k in range(1, BACK + 1):
            rows = slice(k * LOC, (k + 1) * LOC)
            term_send[g, 0, k - 1] = (dk_acc[rows, :] * inv_root).astype(BF16)
            term_send[g, 1, k - 1] = dv_acc[rows, :].astype(BF16)
        for kind in range(2):
            for k in range(BACK, 0, -1):
                @pl.when(c >= k)
                def _(k=k, g=g, kind=kind):
                    term_copy(g, kind, k).start()

    dq_copy = pltpu.make_async_copy(dq_v, dq_hbm, local_sem.at[7])
    dq_copy.start()
    sent.append(dq_copy.wait)

    kg_step(2, 0)
    key_gradient(1)

    def xf_copy(k):
        rows = pl.ds(pl.multiple_of(lax.rem(z + NZ - k, NZ) * LOC, LOC), LOC)
        part = xr.at[t, :, rows, :]
        return remote(part, part, xf_send_sem.at[k], xf_recv_sem.at[k], (c, d, 1 - t))

    def x_forward(k):
        if k == 0:
            for copy in x_own:
                copy.wait()
        else:
            x_copy(k, 0).wait_recv()
            x_copy(k, 1).wait_recv()
        xf_copy(k).start()

    for step in range(3):
        kg_step(step, 1)
    kg_step(3, 0)
    kg_step(3, 1)
    sources = (0, 1, 7, 2, 6, 3, 5, 4)
    x_forward(sources[0])
    sent.extend(kg_copy(s, way, g).wait_send for s, way, g in kg_ring)
    sent.append(lambda: over(0, NZ, lambda k: xf_copy(k).wait_send()))

    for n, k in enumerate(sources):
        if n + 1 < NZ:
            x_forward(sources[n + 1])
        xf_copy(k).wait_recv()
        source = lax.rem(z + NZ - k, NZ)
        tokens = pl.ds(pl.multiple_of(source * LOC, LOC), LOC)
        for i in range(2):
            for h in range(2):
                rows = slice(h * LOC, (h + 1) * LOC)
                term = dot_nn(kgt[source], xr[h, i, tokens, :])
                if n > 0:
                    term = term + gacc[i, :, rows]
                if n + 1 < NZ:
                    gacc[i, :, rows] = term
                else:
                    gtb[i, :, rows] = term.astype(BF16)

    part_rows = LOC // NCTX

    def rs_copy(k):
        p, device = plane_peer(k)
        return remote(
            gtb.at[p // NCTX, pl.ds(pl.multiple_of(lax.rem(p, NCTX) * part_rows, part_rows), part_rows), :],
            rbuf.at[k], rs_send_sem.at[k], rs_recv_sem.at[k], device,
        )

    def rs_start(k, carry):
        rs_copy(k).start()
        return carry

    lax.fori_loop(1, NPLANE, rs_start, 0)

    for g in range(KVH):
        for k in range(1, BACK + 1):
            @pl.when(c + k < NCTX)
            def _(k=k, g=g):
                term_copy(g, 1, k).wait_recv()
                dv_own[g] = dv_own[g] + term_recv[g, 1, k - 1].astype(F32)
        dv_out[:, g * HD:(g + 1) * HD] = dv_own[g].astype(BF16)

    def rs_sum(k, total):
        rs_copy(k).wait_recv()
        return total + rbuf[k].astype(F32)

    sent.append(lambda: over(1, NPLANE, lambda k: rs_copy(k).wait_send()))
    own_rows = pl.ds(pl.multiple_of(c * part_rows, part_rows), part_rows)
    total = lax.fori_loop(1, NPLANE, rs_sum, gtb[xl, own_rows, :].astype(F32))
    gall[own_rows, :] = (total * (1.0 / math.sqrt(NDP * NCTX * LOC))).astype(BF16)

    def ga_copy(k):
        return remote(gall.at[own_rows, :], gall.at[own_rows, :], ga_send_sem.at[k], ga_recv_sem.at[k], ctx_peer(k))

    def ga_start(k, carry):
        ga_copy(k).start()
        return carry

    def ga_wait(k, carry):
        ga_copy(k).wait_recv()
        return carry

    lax.fori_loop(1, NCTX, ga_start, 0)
    for copy in opt_copies:
        copy.wait()
    lax.fori_loop(1, NCTX, ga_wait, 0)

    sent.append(lambda: over(1, NCTX, lambda k: ga_copy(k).wait_send()))
    for h in range(2):
        grad = gall[:, h * LOC:(h + 1) * LOC].astype(F32).T
        grad_out[h] = grad
        nms = adam(grad, opt_v[0, h], opt_v[1, h], opt_v[2, h])[0]
        wb[h] = nms.astype(BF16).reshape(NCTX, part_rows, LOC)

    keeps = [
        pltpu.make_async_copy(wb.at[0], kw_hbm.at[0, d], local_sem.at[8]),
        pltpu.make_async_copy(wb.at[1, c], kw_hbm.at[1, d, c], local_sem.at[9]),
    ]
    for keep in keeps:
        keep.start()

    def zs_copy(k):
        return remote(
            wb.at[1, c], kw_hbm.at[1, d, c], zs_send_sem.at[k], zs_recv_sem.at[k], z_peer(k),
        )

    swap = remote(wb.at[0], kw_hbm.at[0, d], sw_send_sem, sw_recv_sem, (c, (1 - xl) * NZ + z, t))

    def ring_copy(s, way, same, src=None):
        step = 1 if way == 0 else NZ - 1
        zb = lax.rem(z + (NZ - s if way == 0 else s), NZ)
        block = (xl if same else 1 - xl) * NZ + zb
        return remote(
            kw_hbm.at[0, block] if src is None else src, kw_hbm.at[0, block],
            ring_send_sem.at[way, s, int(same)], ring_recv_sem.at[way, s, int(same)], z_peer(step),
        )

    over(1, NZ, lambda k: zs_copy(k).start())
    swap.start()
    ring_copy(0, 0, True, wb.at[0]).start()
    ring_copy(0, 1, True, wb.at[0]).start()
    swap.wait_recv()
    ring_copy(0, 0, False).start()
    ring_copy(0, 1, False).start()
    over(1, NZ, lambda k: zs_copy(k).wait_recv())
    for keep in keeps:
        keep.wait()

    y = c // 2
    x = 2 * lax.rem(c, 2) + xl

    def chip(xx, yy):
        xx, yy = lax.rem(xx, 4), lax.rem(yy, 4)
        return (2 * yy + xx // 2, lax.rem(xx, 2) * NZ + z, t)

    def piece(xx, yy, first):
        xx, yy = lax.rem(xx, 4), lax.rem(yy, 4)
        return kw_hbm.at[1, pl.ds(lax.rem(xx, 2) * NZ + first * (NZ // 2), NZ // 2), 2 * yy + xx // 2]

    def stage1(first, j):
        part = piece(x, y, first)
        device = chip(x + j, y) if first == 0 else chip(x, y + j)
        return remote(part, part, s1_send_sem.at[first, j], s1_recv_sem.at[first, j], device)

    def stage2(first, a, j):
        part = piece(x + 4 - a, y, first) if first == 0 else piece(x, y + 4 - a, first)
        device = chip(x, y + j) if first == 0 else chip(x + j, y)
        return remote(part, part, s2_send_sem.at[first, a, j], s2_recv_sem.at[first, a, j], device)

    ring = [(s, way, same) for s in range(4) for same in (True, False) for way in range(2) if s < 3 or same == (way == 0)]

    def ring_step(step):
        for s, way, same in ring:
            if s == step:
                ring_copy(s, way, same).wait_recv()
                if (s + 1, way, same) in ring:
                    ring_copy(s + 1, way, same).start()

    for j in (2, 1, 3):
        for first in range(2):
            stage1(first, j).start()
    for j in (2, 1, 3):
        for first in range(2):
            stage2(first, 0, j).start()
    ring_step(0)
    for step, a in enumerate((1, 3, 2)):
        for first in range(2):
            stage1(first, a).wait_recv()
            over(1, 4, lambda j: stage2(first, a, j).start())
        ring_step(step + 1)
    for first in range(2):
        for a in range(4):
            over(1, 4, lambda j: stage2(first, a, j).wait_recv())

    sent.append(swap.wait_send)
    sent.append(lambda: over(1, NZ, lambda k: zs_copy(k).wait_send()))
    sent.extend(ring_copy(s, way, same).wait_send for s, way, same in ring)
    for first in range(2):
        sent.append(lambda first=first: over(1, 4, lambda j: stage1(first, j).wait_send()))
        for a in range(4):
            sent.append(lambda first=first, a=a: over(1, 4, lambda j: stage2(first, a, j).wait_send()))

    for wait in sent:
        wait()


def on_device(
    layer_input, queries, keys, values, out_grad, doc_ids, freq_bins, master, moment1, moment2
):
    positions = lax.axis_index("ctx") * LOC + jnp.arange(LOC, dtype=jnp.int32)
    angles = positions.astype(F32)[:, None] * frequencies(freq_bins)[None, :]
    cosine = jnp.cos(angles) * magnitude_scale
    sine = jnp.sin(angles) * magnitude_scale
    cosine = jnp.concatenate([cosine, cosine], axis=1)
    sine = jnp.concatenate([-sine, sine], axis=1)

    any_ = pl.BlockSpec(memory_space=pl.ANY)
    vmem = pl.BlockSpec(memory_space=pltpu.VMEM)
    dma = pltpu.SemaphoreType.DMA
    part_rows = LOC // NCTX
    rows, cols = 2, LOC
    dq, dv, grad, kw = pl.pallas_call(
        kernel,
        out_shape=(
            jax.ShapeDtypeStruct((LOC, KVH * GROUP * HD), BF16),
            jax.ShapeDtypeStruct((LOC, KVH * HD), BF16),
            jax.ShapeDtypeStruct((rows, LOC, cols), F32),
            jax.ShapeDtypeStruct((2, NDP, NCTX, part_rows, cols), BF16),
        ),
        in_specs=[any_, any_, vmem, vmem, vmem, vmem, vmem, any_, any_, any_, any_],
        out_specs=(any_, vmem, vmem, any_),
        scratch_shapes=[
            pltpu.VMEM((LOC, KVH * GROUP * HD), BF16),
            pltpu.VMEM((LOC, KVH * GROUP * HD), BF16),
            pltpu.VMEM((LOC, KVH * GROUP * HD), BF16),
            pltpu.VMEM((KVH, 2, WIN, HD), BF16),
            pltpu.VMEM((HD, WIN), BF16),
            pltpu.VMEM((BACK + 1, 8, LOC), jnp.int32),
            pltpu.VMEM((WIN, LOC), F32),
            pltpu.VMEM((2, LOC, HD), BF16),
            pltpu.VMEM((2, WIN, LOC), F32),
            pltpu.VMEM((2, WIN, LOC), F32),
            pltpu.VMEM((2, WIN, LOC), BF16),
            pltpu.VMEM((2, WIN, LOC), BF16),
            pltpu.VMEM((WIN, HD), F32),
            pltpu.VMEM((WIN, HD), F32),
            pltpu.VMEM((KVH, 2, BACK, LOC, HD), BF16),
            pltpu.VMEM((KVH, 2, BACK, LOC, HD), BF16),
            pltpu.VMEM((KVH, LOC, HD), F32),
            pltpu.VMEM((KVH, LOC, HD), F32),
            pltpu.VMEM((2, 2, NZ * LOC, LOC), BF16),
            pltpu.VMEM((NZ, LOC, LOC), BF16),
            pltpu.VMEM((2, LOC, 2 * LOC), F32),
            pltpu.VMEM((2, LOC, 2 * LOC), BF16),
            pltpu.VMEM((NPLANE, part_rows, 2 * LOC), BF16),
            pltpu.VMEM((LOC, 2 * LOC), BF16),
            pltpu.VMEM((3, 2, LOC, LOC), F32),
            pltpu.VMEM((2, NCTX, part_rows, LOC), BF16),
            dma((10,)),
            dma((BACK,)), dma((BACK,)),
            dma((KVH, BACK)), dma((KVH, BACK)),
            dma((NZ, 2)), dma((NZ, 2)),
            dma((NZ,)), dma((NZ,)),
            dma((KVH, 2, BACK)), dma((KVH, 2, BACK)),
            dma((2, 4, KVH)), dma((2, 4, KVH)),
            dma((NPLANE,)), dma((NPLANE,)),
            dma((NCTX,)), dma((NCTX,)),
            dma, dma,
            dma((2, 4, 2)), dma((2, 4, 2)),
            dma((NZ,)), dma((NZ,)),
            dma((2, 4)), dma((2, 4)),
            dma((2, 4, 4)), dma((2, 4, 4)),
        ],
        compiler_params=pltpu.CompilerParams(
            collective_id=0, has_side_effects=True, vmem_limit_bytes=54 * 1024 * 1024
        ),
    )(
        queries[0], out_grad[0], keys[0], values[0], doc_ids, cosine, sine, layer_input[0],
        master, moment1, moment2,
    )
    new_master, new_moment1, new_moment2 = adam(grad, master, moment1, moment2)
    return (dq[None], dv[None], new_master, new_moment1, new_moment2, kw.reshape(2, NDP * LOC, cols))


def solution(mesh):
    placed = (
        P("dp", "ctx", "tp"),
        P("dp", "ctx", "tp"),
        P("dp", "ctx", "tp"),
        P("dp", "ctx", "tp"),
        P("dp", "ctx", "tp"),
        P("dp", "ctx"),
        P(),
        P(None, "dp", "tp"),
        P(None, "dp", "tp"),
        P(None, "dp", "tp"),
    )
    return jax.shard_map(
        on_device,
        mesh=mesh,
        in_specs=placed,
        out_specs=(
            P("dp", "ctx", "tp"),
            P("dp", "ctx", "tp"),
            P(None, "dp", "tp"),
            P(None, "dp", "tp"),
            P(None, "dp", "tp"),
            P(None, None, "tp"),
        ),
        check_vma=False,
    )
```

```python
import functools
import math

import jax
import jax.numpy as jnp
from jax import lax
from jax.experimental import pallas as pl
from jax.experimental.pallas import tpu as pltpu
from jax.sharding import PartitionSpec as P

HD = 128
BINS = 32
ADAM_STEP = 10
NCTX = 8
NDP = 16
NZ = 8
NPLANE = 16
BACK = 4
LOC = 256
GROUP = 8
KVH = 2
WIN = (BACK + 1) * LOC
CH = 128

rope_base = 10000.0
yarn_factor = 8.0
magnitude_scale = 0.1 * math.log(8.0) + 1.0
beta_first = 0.9
beta_second = 0.95
adam_epsilon = 1e-08
learn_rate = 0.0003
weight_decay = 0.1
inv_root = 1.0 / math.sqrt(HD)
MESH = pl.DeviceIdType.MESH
F32 = jnp.float32
BF16 = jnp.bfloat16


def frequencies(freq_bins):
    pairs = jnp.arange(HD // 2).astype(jnp.float32)
    theta = jnp.exp(pairs * (-2.0 * math.log(rope_base) / HD))
    gamma = freq_bins.astype(jnp.float32) / BINS
    return theta * ((1.0 - gamma) / yarn_factor + gamma)


def dot_nt(a, b):
    return lax.dot_general(a, b, (((1,), (1,)), ((), ())), preferred_element_type=F32)


def dot_nn(a, b):
    return lax.dot_general(a, b, (((1,), (0,)), ((), ())), preferred_element_type=F32)


def adam(grad, master, moment1, moment2):
    new_moment1 = beta_first * moment1 + (1.0 - beta_first) * grad
    new_moment2 = beta_second * moment2 + (1.0 - beta_second) * grad * grad
    first_fix = 1.0 - beta_first**ADAM_STEP
    second_fix = 1.0 - beta_second**ADAM_STEP
    update = new_moment1 / first_fix / (jnp.sqrt(new_moment2 / second_fix) + adam_epsilon)
    return master - learn_rate * (update + weight_decay * master), new_moment1, new_moment2


def rows8(op, value):
    return op(value.reshape(value.shape[0] // 8, 8, value.shape[1]), axis=0)


def kernel(
    q_hbm, og_hbm, k_ref, v_ref, doc_ref, cos_ref, sin_ref, x_hbm, ms_hbm, m1_hbm, m2_hbm,
    dq_hbm, dv_out, grad_out, kw_hbm,
    q_v, og_v, dq_v, kv, kt, docs, bias, rq_ref, t_ref, dp_ref, p_ref, ds_ref, dk_acc, dv_acc,
    term_send, term_recv, kg_own, dv_own, xr, kgt, gacc, gtb, rbuf, gall, opt_v, wb,
    local_sem, doc_send_sem, doc_recv_sem, kv_send_sem, kv_recv_sem, x_send_sem, x_recv_sem,
    xf_send_sem, xf_recv_sem, term_send_sem, term_recv_sem, kg_send_sem, kg_recv_sem,
    rs_send_sem, rs_recv_sem, ga_send_sem, ga_recv_sem,
    sw_send_sem, sw_recv_sem, ring_send_sem, ring_recv_sem,
    zs_send_sem, zs_recv_sem, s1_send_sem, s1_recv_sem, s2_send_sem, s2_recv_sem,
):
    c = lax.axis_index("ctx")
    d = lax.axis_index("dp")
    t = lax.axis_index("tp")
    z = lax.rem(d, NZ)
    xl = d // NZ
    me_p = xl * NCTX + c

    def z_peer(k):
        return (c, xl * NZ + lax.rem(z + k, NZ), t)

    def plane_peer(k):
        p = lax.rem(me_p + k, NPLANE)
        return p, (lax.rem(p, NCTX), (p // NCTX) * NZ + z, t)

    def ctx_peer(k):
        return (lax.rem(c + k, NCTX), d, t)

    def remote(src, dst, ssem, rsem, device):
        return pltpu.make_async_remote_copy(
            src_ref=src, dst_ref=dst, send_sem=ssem, recv_sem=rsem,
            device_id=device, device_id_type=MESH,
        )

    sent = []

    def over(low, high, one):
        def step(k, carry):
            one(k)
            return carry

        lax.fori_loop(low, high, step, 0)

    q_copy = pltpu.make_async_copy(q_hbm, q_v, local_sem.at[0])
    og_copy = pltpu.make_async_copy(og_hbm, og_v, local_sem.at[1])
    opt_copies = [
        pltpu.make_async_copy(src, opt_v.at[i], local_sem.at[2 + i])
        for i, src in enumerate((ms_hbm, m1_hbm, m2_hbm))
    ]
    x_own = [
        pltpu.make_async_copy(
            x_hbm.at[:, pl.ds(pl.multiple_of((i * NZ + z) * LOC, LOC), LOC)],
            xr.at[t, i, pl.ds(pl.multiple_of(z * LOC, LOC), LOC), :],
            local_sem.at[5 + i],
        )
        for i in range(2)
    ]
    for copy in [q_copy, og_copy] + opt_copies + x_own:
        copy.start()

    barrier = pltpu.get_barrier_semaphore()

    def greet_z(k, carry):
        pl.semaphore_signal(barrier, inc=1, device_id=z_peer(k), device_id_type=MESH)
        return carry

    def greet_plane(k, carry):
        pl.semaphore_signal(barrier, inc=1, device_id=plane_peer(k)[1], device_id_type=MESH)
        return carry

    lax.fori_loop(1, NZ, greet_z, 0)
    lax.fori_loop(1, NPLANE, greet_plane, 0)
    pl.semaphore_signal(barrier, inc=1, device_id=(c, d, 1 - t), device_id_type=MESH)

    cosv = cos_ref[...]
    sinv = sin_ref[...]
    for g in range(KVH):
        kh = k_ref[:, g * HD:(g + 1) * HD].astype(F32)
        kv[g, 0, 0:LOC, :] = (kh * cosv + pltpu.roll(kh, HD // 2, 1) * sinv).astype(BF16)
        kv[g, 1, 0:LOC, :] = v_ref[:, g * HD:(g + 1) * HD]
    docs[0] = jnp.broadcast_to(doc_ref[...], (8, LOC))

    pl.semaphore_wait(barrier, (NZ - 1) + (NPLANE - 1) + 1)

    def doc_copy(k):
        return remote(docs.at[0], docs.at[k], doc_send_sem.at[k - 1], doc_recv_sem.at[k - 1], ctx_peer(k))

    def kv_copy(g, k):
        return remote(
            kv.at[g, :, pl.ds(0, LOC), :], kv.at[g, :, pl.ds(k * LOC, LOC), :],
            kv_send_sem.at[g, k - 1], kv_recv_sem.at[g, k - 1], ctx_peer(k),
        )

    for k in range(BACK, 0, -1):
        @pl.when(c + k < NCTX)
        def _(k=k):
            doc_copy(k).start()
            kv_copy(0, k).start()

    def kv_sent():
        for k in range(1, BACK + 1):
            @pl.when(c + k < NCTX)
            def _(k=k):
                doc_copy(k).wait_send()
                for g in range(KVH):
                    kv_copy(g, k).wait_send()

    sent.append(kv_sent)

    def x_copy(k, i):
        zd = lax.rem(z + k, NZ)
        return remote(
            x_hbm.at[:, pl.ds(pl.multiple_of((i * NZ + zd) * LOC, LOC), LOC)],
            xr.at[t, i, pl.ds(pl.multiple_of(z * LOC, LOC), LOC), :],
            x_send_sem.at[k, i], x_recv_sem.at[k, i], z_peer(k),
        )

    def x_start(k, carry):
        x_copy(k, 0).start()
        x_copy(k, 1).start()
        return carry

    def x_sent(k):
        x_copy(k, 0).wait_send()
        x_copy(k, 1).wait_send()

    sent.append(lambda: over(1, NZ, x_sent))

    lax.fori_loop(1, NZ, x_start, 0)

    for k in range(1, BACK + 1):
        @pl.when(c + k < NCTX)
        def _(k=k):
            kv_copy(1, k).start()

        @pl.when(c < k)
        def _(k=k):
            kv[:, :, k * LOC:(k + 1) * LOC, :] = jnp.zeros((KVH, 2, LOC, HD), BF16)
            docs[k] = jnp.full((8, LOC), 127, jnp.int32)

    for k in range(1, BACK + 1):
        @pl.when(c >= k)
        def _(k=k):
            doc_copy(k).wait_recv()
    own_docs = doc_ref[...]
    window_start = jnp.maximum(c - BACK, 0) * LOC
    start = jnp.zeros((1, LOC), F32)
    for doc in range(1, 4):
        below = jnp.zeros((8, LOC), F32)
        for k in range(BACK + 1):
            below = below + (docs[k] < doc).astype(F32)
        count = jnp.sum(below[0:1], axis=1, keepdims=True)
        start = jnp.where(own_docs == doc, count, start)
    start = start.astype(jnp.int32) + window_start
    query_pos = c * LOC + lax.broadcasted_iota(jnp.int32, (1, LOC), 1)
    for k in range(BACK + 1):
        key_pos = (c - k) * LOC + lax.broadcasted_iota(jnp.int32, (LOC, LOC), 0)
        seen = (key_pos <= query_pos) & (key_pos >= start)
        bias[k * LOC:(k + 1) * LOC, :] = jnp.where(seen, 0.0, -jnp.inf)

    q_copy.wait()
    og_copy.wait()
    scale2 = inv_root * math.log2(math.e)
    chunks = [slice(j * CH, (j + 1) * CH) for j in range(WIN // CH)]

    def term_copy(g, kind, k):
        return remote(
            term_send.at[g, kind, k - 1], term_recv.at[g, kind, k - 1],
            term_send_sem.at[g, kind, k - 1], term_recv_sem.at[g, kind, k - 1],
            ctx_peer(NCTX - k),
        )

    def term_start(g, kind):
        for k in range(BACK, 0, -1):
            @pl.when(c >= k)
            def _(k=k):
                term_copy(g, kind, k).start()

    def term_sent(g):
        for k in range(1, BACK + 1):
            @pl.when(c >= k)
            def _(k=k):
                for kind in range(2):
                    term_copy(g, kind, k).wait_send()

    sent.append(lambda: term_sent(0))
    sent.append(lambda: term_sent(1))
    def kg_copy(s, way, g):
        zb = lax.rem(z + (NZ - s if way == 0 else s), NZ)
        part = kgt.at[zb, pl.ds(g * HD, HD), :]
        return remote(
            part, part, kg_send_sem.at[way, s, g], kg_recv_sem.at[way, s, g],
            z_peer(1 if way == 0 else NZ - 1),
        )

    kg_ring = [(s, way, g) for s in range(4) for g in range(KVH) for way in range(2) if s < 3 or g == way]

    def key_gradient(g):
        for k in range(1, BACK + 1):
            @pl.when(c + k < NCTX)
            def _(k=k):
                term_copy(g, 0, k).wait_recv()
                kg_own[g] = kg_own[g] + term_recv[g, 0, k - 1].astype(F32)
        kg = kg_own[g]
        kg = kg * cos_ref[...] - pltpu.roll(kg, HD // 2, 1) * sin_ref[...]
        kgt[z, pl.ds(g * HD, HD), :] = kg.T.astype(BF16)
        for way in range(2):
            kg_copy(0, way, g).start()

    def kg_step(step, head):
        for s, way, g in kg_ring:
            if s == step and g == head:
                kg_copy(s, way, g).wait_recv()
                if (s + 1, way, g) in kg_ring:
                    kg_copy(s + 1, way, g).start()

    for g in range(KVH):
        for k in range(1, BACK + 1):
            @pl.when(c >= k)
            def _(k=k, g=g):
                kv_copy(g, k).wait_recv()
        for sl in chunks:
            kt[:, sl] = kv[g, 0, sl, :].astype(F32).T.astype(BF16)
        dk_acc[...] = jnp.zeros_like(dk_acc)
        dv_acc[...] = jnp.zeros_like(dv_acc)

        def head_columns(h, g=g):
            return pl.ds(pl.multiple_of((g * GROUP + h) * HD, HD), HD)

        def products(h, b, g=g):
            qh = q_v[:, head_columns(h)].astype(F32)
            rq = (qh * cos_ref[...] + pltpu.roll(qh, HD // 2, 1) * sin_ref[...]).astype(BF16)
            rq_ref[b] = rq
            t_ref[b] = dot_nt(kv[g, 0], rq)
            dp_ref[b] = dot_nt(kv[g, 1], og_v[:, head_columns(h)])

        def softmax(b):
            top = None
            for sl in chunks:
                score = t_ref[b, sl, :] * scale2 + bias[sl, :]
                t_ref[b, sl, :] = score
                part = rows8(jnp.max, score)
                top = part if top is None else jnp.maximum(top, part)
            top = jnp.max(top, axis=0, keepdims=True)
            total = jnp.zeros((8, LOC), F32)
            mixed = jnp.zeros((8, LOC), F32)
            for sl in chunks:
                e = jnp.exp2(t_ref[b, sl, :] - top)
                t_ref[b, sl, :] = e
                total = total + rows8(jnp.sum, e)
                mixed = mixed + rows8(jnp.sum, e * dp_ref[b, sl, :])
            inv_total = 1.0 / jnp.sum(total, axis=0, keepdims=True)
            delta = jnp.sum(mixed, axis=0, keepdims=True) * inv_total
            for sl in chunks:
                p = t_ref[b, sl, :] * inv_total
                ds_ref[b, sl, :] = (p * (dp_ref[b, sl, :] - delta)).astype(BF16)
                p_ref[b, sl, :] = p.astype(BF16)

        def gradients(h, b):
            dk_acc[...] += dot_nn(ds_ref[b], rq_ref[b])
            dv_acc[...] += dot_nn(p_ref[b], og_v[:, head_columns(h)])
            dq = dot_nn(kt[...], ds_ref[b]).T * inv_root
            dq = dq * cos_ref[...] - pltpu.roll(dq, HD // 2, 1) * sin_ref[...]
            dq_v[:, head_columns(h)] = dq.astype(BF16)

        def two_heads(i, carry, g=g):
            for b in range(2):
                products(2 * i + b, b)
            for b in range(2):
                softmax(b)
            for b in range(2):
                gradients(2 * i + b, b)
            return carry

        lax.fori_loop(0, GROUP // 2, two_heads, 0)

        kg_own[g] = dk_acc[0:LOC, :] * inv_root
        dv_own[g] = dv_acc[0:LOC, :]
        for k in range(1, BACK + 1):
            rows = slice(k * LOC, (k + 1) * LOC)
            term_send[g, 0, k - 1] = (dk_acc[rows, :] * inv_root).astype(BF16)
            term_send[g, 1, k - 1] = dv_acc[rows, :].astype(BF16)
        term_start(g, 0)
        if g == 0:
            term_start(g, 1)

    dq_copy = pltpu.make_async_copy(dq_v, dq_hbm, local_sem.at[7])
    dq_copy.start()
    sent.append(dq_copy.wait)

    key_gradient(0)
    kg_step(0, 0)
    kg_step(1, 0)
    key_gradient(1)
    term_start(1, 1)
    kg_step(2, 0)

    def xf_copy(k):
        rows = pl.ds(pl.multiple_of(lax.rem(z + NZ - k, NZ) * LOC, LOC), LOC)
        part = xr.at[t, :, rows, :]
        return remote(part, part, xf_send_sem.at[k], xf_recv_sem.at[k], (c, d, 1 - t))

    def x_forward(k):
        if k == 0:
            for copy in x_own:
                copy.wait()
        else:
            x_copy(k, 0).wait_recv()
            x_copy(k, 1).wait_recv()
        xf_copy(k).start()

    for step in range(3):
        kg_step(step, 1)
    kg_step(3, 0)
    kg_step(3, 1)
    sources = (0, 1, 7, 2, 6, 3, 5, 4)
    x_forward(sources[0])
    sent.extend(kg_copy(s, way, g).wait_send for s, way, g in kg_ring)
    sent.append(lambda: over(0, NZ, lambda k: xf_copy(k).wait_send()))

    for n, k in enumerate(sources):
        if n + 1 < NZ:
            x_forward(sources[n + 1])
        xf_copy(k).wait_recv()
        source = lax.rem(z + NZ - k, NZ)
        tokens = pl.ds(pl.multiple_of(source * LOC, LOC), LOC)
        for i in range(2):
            for h in range(2):
                rows = slice(h * LOC, (h + 1) * LOC)
                term = dot_nn(kgt[source], xr[h, i, tokens, :])
                if n > 0:
                    term = term + gacc[i, :, rows]
                if n + 1 < NZ:
                    gacc[i, :, rows] = term
                else:
                    gtb[i, :, rows] = term.astype(BF16)

    part_rows = LOC // NCTX

    def rs_copy(k):
        p, device = plane_peer(k)
        return remote(
            gtb.at[p // NCTX, pl.ds(pl.multiple_of(lax.rem(p, NCTX) * part_rows, part_rows), part_rows), :],
            rbuf.at[k], rs_send_sem.at[k], rs_recv_sem.at[k], device,
        )

    def rs_start(k, carry):
        rs_copy(k).start()
        return carry

    lax.fori_loop(1, NPLANE, rs_start, 0)

    for g in range(KVH):
        for k in range(1, BACK + 1):
            @pl.when(c + k < NCTX)
            def _(k=k, g=g):
                term_copy(g, 1, k).wait_recv()
                dv_own[g] = dv_own[g] + term_recv[g, 1, k - 1].astype(F32)
        dv_out[:, g * HD:(g + 1) * HD] = dv_own[g].astype(BF16)

    def rs_sum(k, total):
        rs_copy(k).wait_recv()
        return total + rbuf[k].astype(F32)

    sent.append(lambda: over(1, NPLANE, lambda k: rs_copy(k).wait_send()))
    own_rows = pl.ds(pl.multiple_of(c * part_rows, part_rows), part_rows)
    total = lax.fori_loop(1, NPLANE, rs_sum, gtb[xl, own_rows, :].astype(F32))
    gall[own_rows, :] = (total * (1.0 / math.sqrt(NDP * NCTX * LOC))).astype(BF16)

    def ga_copy(k):
        return remote(gall.at[own_rows, :], gall.at[own_rows, :], ga_send_sem.at[k], ga_recv_sem.at[k], ctx_peer(k))

    def ga_start(k, carry):
        ga_copy(k).start()
        return carry

    def ga_wait(k, carry):
        ga_copy(k).wait_recv()
        return carry

    lax.fori_loop(1, NCTX, ga_start, 0)
    for copy in opt_copies:
        copy.wait()
    lax.fori_loop(1, NCTX, ga_wait, 0)

    sent.append(lambda: over(1, NCTX, lambda k: ga_copy(k).wait_send()))
    for h in range(2):
        grad = gall[:, h * LOC:(h + 1) * LOC].astype(F32).T
        grad_out[h] = grad
        nms = adam(grad, opt_v[0, h], opt_v[1, h], opt_v[2, h])[0]
        wb[h] = nms.astype(BF16).reshape(NCTX, part_rows, LOC)

    keeps = [
        pltpu.make_async_copy(wb.at[0], kw_hbm.at[0, d], local_sem.at[8]),
        pltpu.make_async_copy(wb.at[1, c], kw_hbm.at[1, d, c], local_sem.at[9]),
    ]
    for keep in keeps:
        keep.start()

    def zs_copy(k):
        return remote(
            wb.at[1, c], kw_hbm.at[1, d, c], zs_send_sem.at[k], zs_recv_sem.at[k], z_peer(k),
        )

    swap = remote(wb.at[0], kw_hbm.at[0, d], sw_send_sem, sw_recv_sem, (c, (1 - xl) * NZ + z, t))

    def ring_copy(s, way, same, src=None):
        step = 1 if way == 0 else NZ - 1
        zb = lax.rem(z + (NZ - s if way == 0 else s), NZ)
        block = (xl if same else 1 - xl) * NZ + zb
        return remote(
            kw_hbm.at[0, block] if src is None else src, kw_hbm.at[0, block],
            ring_send_sem.at[way, s, int(same)], ring_recv_sem.at[way, s, int(same)], z_peer(step),
        )

    over(1, NZ, lambda k: zs_copy(k).start())
    swap.start()
    ring_copy(0, 0, True, wb.at[0]).start()
    ring_copy(0, 1, True, wb.at[0]).start()
    swap.wait_recv()
    ring_copy(0, 0, False).start()
    ring_copy(0, 1, False).start()
    over(1, NZ, lambda k: zs_copy(k).wait_recv())
    for keep in keeps:
        keep.wait()

    y = c // 2
    x = 2 * lax.rem(c, 2) + xl

    def chip(xx, yy):
        xx, yy = lax.rem(xx, 4), lax.rem(yy, 4)
        return (2 * yy + xx // 2, lax.rem(xx, 2) * NZ + z, t)

    def piece(xx, yy, first):
        xx, yy = lax.rem(xx, 4), lax.rem(yy, 4)
        return kw_hbm.at[1, pl.ds(lax.rem(xx, 2) * NZ + first * (NZ // 2), NZ // 2), 2 * yy + xx // 2]

    def stage1(first, j):
        part = piece(x, y, first)
        device = chip(x + j, y) if first == 0 else chip(x, y + j)
        return remote(part, part, s1_send_sem.at[first, j], s1_recv_sem.at[first, j], device)

    def stage2(first, a, j):
        part = piece(x + 4 - a, y, first) if first == 0 else piece(x, y + 4 - a, first)
        device = chip(x, y + j) if first == 0 else chip(x + j, y)
        return remote(part, part, s2_send_sem.at[first, a, j], s2_recv_sem.at[first, a, j], device)

    ring = [(s, way, same) for s in range(4) for same in (True, False) for way in range(2) if s < 3 or same == (way == 0)]

    def ring_step(step):
        for s, way, same in ring:
            if s == step:
                ring_copy(s, way, same).wait_recv()
                if (s + 1, way, same) in ring:
                    ring_copy(s + 1, way, same).start()

    for j in (2, 1, 3):
        for first in range(2):
            stage1(first, j).start()
    for j in (2, 1, 3):
        for first in range(2):
            stage2(first, 0, j).start()
    ring_step(0)
    for step, a in enumerate((1, 3, 2)):
        for first in range(2):
            stage1(first, a).wait_recv()
            over(1, 4, lambda j: stage2(first, a, j).start())
        ring_step(step + 1)
    for first in range(2):
        for a in range(4):
            over(1, 4, lambda j: stage2(first, a, j).wait_recv())

    sent.append(swap.wait_send)
    sent.append(lambda: over(1, NZ, lambda k: zs_copy(k).wait_send()))
    sent.extend(ring_copy(s, way, same).wait_send for s, way, same in ring)
    for first in range(2):
        sent.append(lambda first=first: over(1, 4, lambda j: stage1(first, j).wait_send()))
        for a in range(4):
            sent.append(lambda first=first, a=a: over(1, 4, lambda j: stage2(first, a, j).wait_send()))

    for wait in sent:
        wait()


def on_device(
    layer_input, queries, keys, values, out_grad, doc_ids, freq_bins, master, moment1, moment2
):
    positions = lax.axis_index("ctx") * LOC + jnp.arange(LOC, dtype=jnp.int32)
    angles = positions.astype(F32)[:, None] * frequencies(freq_bins)[None, :]
    cosine = jnp.cos(angles) * magnitude_scale
    sine = jnp.sin(angles) * magnitude_scale
    cosine = jnp.concatenate([cosine, cosine], axis=1)
    sine = jnp.concatenate([-sine, sine], axis=1)

    any_ = pl.BlockSpec(memory_space=pl.ANY)
    vmem = pl.BlockSpec(memory_space=pltpu.VMEM)
    dma = pltpu.SemaphoreType.DMA
    part_rows = LOC // NCTX
    rows, cols = 2, LOC
    dq, dv, grad, kw = pl.pallas_call(
        kernel,
        out_shape=(
            jax.ShapeDtypeStruct((LOC, KVH * GROUP * HD), BF16),
            jax.ShapeDtypeStruct((LOC, KVH * HD), BF16),
            jax.ShapeDtypeStruct((rows, LOC, cols), F32),
            jax.ShapeDtypeStruct((2, NDP, NCTX, part_rows, cols), BF16),
        ),
        in_specs=[any_, any_, vmem, vmem, vmem, vmem, vmem, any_, any_, any_, any_],
        out_specs=(any_, vmem, vmem, any_),
        scratch_shapes=[
            pltpu.VMEM((LOC, KVH * GROUP * HD), BF16),
            pltpu.VMEM((LOC, KVH * GROUP * HD), BF16),
            pltpu.VMEM((LOC, KVH * GROUP * HD), BF16),
            pltpu.VMEM((KVH, 2, WIN, HD), BF16),
            pltpu.VMEM((HD, WIN), BF16),
            pltpu.VMEM((BACK + 1, 8, LOC), jnp.int32),
            pltpu.VMEM((WIN, LOC), F32),
            pltpu.VMEM((2, LOC, HD), BF16),
            pltpu.VMEM((2, WIN, LOC), F32),
            pltpu.VMEM((2, WIN, LOC), F32),
            pltpu.VMEM((2, WIN, LOC), BF16),
            pltpu.VMEM((2, WIN, LOC), BF16),
            pltpu.VMEM((WIN, HD), F32),
            pltpu.VMEM((WIN, HD), F32),
            pltpu.VMEM((KVH, 2, BACK, LOC, HD), BF16),
            pltpu.VMEM((KVH, 2, BACK, LOC, HD), BF16),
            pltpu.VMEM((KVH, LOC, HD), F32),
            pltpu.VMEM((KVH, LOC, HD), F32),
            pltpu.VMEM((2, 2, NZ * LOC, LOC), BF16),
            pltpu.VMEM((NZ, LOC, LOC), BF16),
            pltpu.VMEM((2, LOC, 2 * LOC), F32),
            pltpu.VMEM((2, LOC, 2 * LOC), BF16),
            pltpu.VMEM((NPLANE, part_rows, 2 * LOC), BF16),
            pltpu.VMEM((LOC, 2 * LOC), BF16),
            pltpu.VMEM((3, 2, LOC, LOC), F32),
            pltpu.VMEM((2, NCTX, part_rows, LOC), BF16),
            dma((10,)),
            dma((BACK,)), dma((BACK,)),
            dma((KVH, BACK)), dma((KVH, BACK)),
            dma((NZ, 2)), dma((NZ, 2)),
            dma((NZ,)), dma((NZ,)),
            dma((KVH, 2, BACK)), dma((KVH, 2, BACK)),
            dma((2, 4, KVH)), dma((2, 4, KVH)),
            dma((NPLANE,)), dma((NPLANE,)),
            dma((NCTX,)), dma((NCTX,)),
            dma, dma,
            dma((2, 4, 2)), dma((2, 4, 2)),
            dma((NZ,)), dma((NZ,)),
            dma((2, 4)), dma((2, 4)),
            dma((2, 4, 4)), dma((2, 4, 4)),
        ],
        compiler_params=pltpu.CompilerParams(
            collective_id=0, has_side_effects=True, vmem_limit_bytes=54 * 1024 * 1024
        ),
    )(
        queries[0], out_grad[0], keys[0], values[0], doc_ids, cosine, sine, layer_input[0],
        master, moment1, moment2,
    )
    new_master, new_moment1, new_moment2 = adam(grad, master, moment1, moment2)
    return (dq[None], dv[None], new_master, new_moment1, new_moment2, kw.reshape(2, NDP * LOC, cols))


def solution(mesh):
    placed = (
        P("dp", "ctx", "tp"),
        P("dp", "ctx", "tp"),
        P("dp", "ctx", "tp"),
        P("dp", "ctx", "tp"),
        P("dp", "ctx", "tp"),
        P("dp", "ctx"),
        P(),
        P(None, "dp", "tp"),
        P(None, "dp", "tp"),
        P(None, "dp", "tp"),
    )
    return jax.shard_map(
        on_device,
        mesh=mesh,
        in_specs=placed,
        out_specs=(
            P("dp", "ctx", "tp"),
            P("dp", "ctx", "tp"),
            P(None, "dp", "tp"),
            P(None, "dp", "tp"),
            P(None, "dp", "tp"),
            P(None, None, "tp"),
        ),
        check_vma=False,
    )
```

```python
import functools
import math

import jax
import jax.numpy as jnp
from jax import lax
from jax.experimental import pallas as pl
from jax.experimental.pallas import tpu as pltpu
from jax.sharding import PartitionSpec as P

HD = 128
BINS = 32
ADAM_STEP = 10
NCTX = 8
NDP = 16
NZ = 8
NPLANE = 16
BACK = 4
LOC = 256
GROUP = 8
KVH = 2
WIN = (BACK + 1) * LOC
CH = 128

rope_base = 10000.0
yarn_factor = 8.0
magnitude_scale = 0.1 * math.log(8.0) + 1.0
beta_first = 0.9
beta_second = 0.95
adam_epsilon = 1e-08
learn_rate = 0.0003
weight_decay = 0.1
inv_root = 1.0 / math.sqrt(HD)
MESH = pl.DeviceIdType.MESH
F32 = jnp.float32
BF16 = jnp.bfloat16


def frequencies(freq_bins):
    pairs = jnp.arange(HD // 2).astype(jnp.float32)
    theta = jnp.exp(pairs * (-2.0 * math.log(rope_base) / HD))
    gamma = freq_bins.astype(jnp.float32) / BINS
    return theta * ((1.0 - gamma) / yarn_factor + gamma)


def dot_nt(a, b):
    return lax.dot_general(a, b, (((1,), (1,)), ((), ())), preferred_element_type=F32)


def dot_nn(a, b):
    return lax.dot_general(a, b, (((1,), (0,)), ((), ())), preferred_element_type=F32)


def adam(grad, master, moment1, moment2):
    new_moment1 = beta_first * moment1 + (1.0 - beta_first) * grad
    new_moment2 = beta_second * moment2 + (1.0 - beta_second) * grad * grad
    first_fix = 1.0 - beta_first**ADAM_STEP
    second_fix = 1.0 - beta_second**ADAM_STEP
    update = new_moment1 / first_fix / (jnp.sqrt(new_moment2 / second_fix) + adam_epsilon)
    return master - learn_rate * (update + weight_decay * master), new_moment1, new_moment2


def rows8(op, value):
    return op(value.reshape(value.shape[0] // 8, 8, value.shape[1]), axis=0)


def kernel(
    q_hbm, og_hbm, k_ref, v_ref, doc_ref, cos_ref, sin_ref, x_hbm, ms_hbm, m1_hbm, m2_hbm,
    dq_hbm, dv_out, grad_out, kw_hbm,
    q_v, og_v, dq_v, kv, kt, docs, bias, rq_ref, t_ref, dp_ref, p_ref, ds_ref, dk_acc, dv_acc,
    term_send, term_recv, kg_own, dv_own, xr, kgt, gacc, gtb, rbuf, gall, opt_v, wb,
    local_sem, doc_send_sem, doc_recv_sem, kv_send_sem, kv_recv_sem, x_send_sem, x_recv_sem,
    xf_send_sem, xf_recv_sem, term_send_sem, term_recv_sem, kg_send_sem, kg_recv_sem,
    rs_send_sem, rs_recv_sem, ga_send_sem, ga_recv_sem,
    sw_send_sem, sw_recv_sem, ring_send_sem, ring_recv_sem,
    zs_send_sem, zs_recv_sem, s1_send_sem, s1_recv_sem, s2_send_sem, s2_recv_sem,
):
    c = lax.axis_index("ctx")
    d = lax.axis_index("dp")
    t = lax.axis_index("tp")
    z = lax.rem(d, NZ)
    xl = d // NZ
    me_p = xl * NCTX + c

    def z_peer(k):
        return (c, xl * NZ + lax.rem(z + k, NZ), t)

    def plane_peer(k):
        p = lax.rem(me_p + k, NPLANE)
        return p, (lax.rem(p, NCTX), (p // NCTX) * NZ + z, t)

    def ctx_peer(k):
        return (lax.rem(c + k, NCTX), d, t)

    def remote(src, dst, ssem, rsem, device):
        return pltpu.make_async_remote_copy(
            src_ref=src, dst_ref=dst, send_sem=ssem, recv_sem=rsem,
            device_id=device, device_id_type=MESH,
        )

    sent = []

    def over(low, high, one):
        def step(k, carry):
            one(k)
            return carry

        lax.fori_loop(low, high, step, 0)

    q_copy = pltpu.make_async_copy(q_hbm, q_v, local_sem.at[0])
    og_copy = pltpu.make_async_copy(og_hbm, og_v, local_sem.at[1])
    opt_copies = [
        pltpu.make_async_copy(src, opt_v.at[i], local_sem.at[2 + i])
        for i, src in enumerate((ms_hbm, m1_hbm, m2_hbm))
    ]
    x_own = [
        pltpu.make_async_copy(
            x_hbm.at[:, pl.ds(pl.multiple_of((i * NZ + z) * LOC, LOC), LOC)],
            xr.at[t, i, pl.ds(pl.multiple_of(z * LOC, LOC), LOC), :],
            local_sem.at[5 + i],
        )
        for i in range(2)
    ]
    for copy in [q_copy, og_copy] + opt_copies + x_own:
        copy.start()

    barrier = pltpu.get_barrier_semaphore()

    def greet_z(k, carry):
        pl.semaphore_signal(barrier, inc=1, device_id=z_peer(k), device_id_type=MESH)
        return carry

    def greet_plane(k, carry):
        pl.semaphore_signal(barrier, inc=1, device_id=plane_peer(k)[1], device_id_type=MESH)
        return carry

    lax.fori_loop(1, NZ, greet_z, 0)
    lax.fori_loop(1, NPLANE, greet_plane, 0)
    pl.semaphore_signal(barrier, inc=1, device_id=(c, d, 1 - t), device_id_type=MESH)

    cosv = cos_ref[...]
    sinv = sin_ref[...]
    for g in range(KVH):
        kh = k_ref[:, g * HD:(g + 1) * HD].astype(F32)
        kv[g, 0, 0:LOC, :] = (kh * cosv + pltpu.roll(kh, HD // 2, 1) * sinv).astype(BF16)
        kv[g, 1, 0:LOC, :] = v_ref[:, g * HD:(g + 1) * HD]
    docs[0] = jnp.broadcast_to(doc_ref[...], (8, LOC))

    pl.semaphore_wait(barrier, (NZ - 1) + (NPLANE - 1) + 1)

    def doc_copy(k):
        return remote(docs.at[0], docs.at[k], doc_send_sem.at[k - 1], doc_recv_sem.at[k - 1], ctx_peer(k))

    def kv_copy(g, k):
        return remote(
            kv.at[g, :, pl.ds(0, LOC), :], kv.at[g, :, pl.ds(k * LOC, LOC), :],
            kv_send_sem.at[g, k - 1], kv_recv_sem.at[g, k - 1], ctx_peer(k),
        )

    for k in range(BACK, 0, -1):
        @pl.when(c + k < NCTX)
        def _(k=k):
            doc_copy(k).start()
            kv_copy(0, k).start()

    def kv_sent():
        for k in range(1, BACK + 1):
            @pl.when(c + k < NCTX)
            def _(k=k):
                doc_copy(k).wait_send()
                for g in range(KVH):
                    kv_copy(g, k).wait_send()

    sent.append(kv_sent)

    def x_copy(k, i):
        zd = lax.rem(z + k, NZ)
        return remote(
            x_hbm.at[:, pl.ds(pl.multiple_of((i * NZ + zd) * LOC, LOC), LOC)],
            xr.at[t, i, pl.ds(pl.multiple_of(z * LOC, LOC), LOC), :],
            x_send_sem.at[k, i], x_recv_sem.at[k, i], z_peer(k),
        )

    def x_start(k, carry):
        x_copy(k, 0).start()
        x_copy(k, 1).start()
        return carry

    def x_sent(k):
        x_copy(k, 0).wait_send()
        x_copy(k, 1).wait_send()

    sent.append(lambda: over(1, NZ, x_sent))

    lax.fori_loop(1, NZ, x_start, 0)

    for k in range(1, BACK + 1):
        @pl.when(c + k < NCTX)
        def _(k=k):
            kv_copy(1, k).start()

        @pl.when(c < k)
        def _(k=k):
            kv[:, :, k * LOC:(k + 1) * LOC, :] = jnp.zeros((KVH, 2, LOC, HD), BF16)
            docs[k] = jnp.full((8, LOC), 127, jnp.int32)

    for k in range(1, BACK + 1):
        @pl.when(c >= k)
        def _(k=k):
            doc_copy(k).wait_recv()
    own_docs = doc_ref[...]
    window_start = jnp.maximum(c - BACK, 0) * LOC
    start = jnp.zeros((1, LOC), F32)
    for doc in range(1, 4):
        below = jnp.zeros((8, LOC), F32)
        for k in range(BACK + 1):
            below = below + (docs[k] < doc).astype(F32)
        count = jnp.sum(below[0:1], axis=1, keepdims=True)
        start = jnp.where(own_docs == doc, count, start)
    start = start.astype(jnp.int32) + window_start
    query_pos = c * LOC + lax.broadcasted_iota(jnp.int32, (1, LOC), 1)
    for k in range(BACK + 1):
        key_pos = (c - k) * LOC + lax.broadcasted_iota(jnp.int32, (LOC, LOC), 0)
        seen = (key_pos <= query_pos) & (key_pos >= start)
        bias[k * LOC:(k + 1) * LOC, :] = jnp.where(seen, 0.0, -jnp.inf)

    q_copy.wait()
    og_copy.wait()
    scale2 = inv_root * math.log2(math.e)
    chunks = [slice(j * CH, (j + 1) * CH) for j in range(WIN // CH)]

    def term_copy(g, kind, k):
        return remote(
            term_send.at[g, kind, k - 1], term_recv.at[g, kind, k - 1],
            term_send_sem.at[g, kind, k - 1], term_recv_sem.at[g, kind, k - 1],
            ctx_peer(NCTX - k),
        )

    def term_sent(g):
        for k in range(1, BACK + 1):
            @pl.when(c >= k)
            def _(k=k):
                for kind in range(2):
                    term_copy(g, kind, k).wait_send()

    sent.append(lambda: term_sent(0))
    sent.append(lambda: term_sent(1))
    for g in range(KVH):
        for k in range(1, BACK + 1):
            @pl.when(c >= k)
            def _(k=k, g=g):
                kv_copy(g, k).wait_recv()
        for sl in chunks:
            kt[:, sl] = kv[g, 0, sl, :].astype(F32).T.astype(BF16)
        dk_acc[...] = jnp.zeros_like(dk_acc)
        dv_acc[...] = jnp.zeros_like(dv_acc)

        def head_columns(h, g=g):
            return pl.ds(pl.multiple_of((g * GROUP + h) * HD, HD), HD)

        def products(h, b, g=g):
            qh = q_v[:, head_columns(h)].astype(F32)
            rq = (qh * cos_ref[...] + pltpu.roll(qh, HD // 2, 1) * sin_ref[...]).astype(BF16)
            rq_ref[b] = rq
            t_ref[b] = dot_nt(kv[g, 0], rq)
            dp_ref[b] = dot_nt(kv[g, 1], og_v[:, head_columns(h)])

        def softmax(b):
            top = None
            for sl in chunks:
                score = t_ref[b, sl, :] * scale2 + bias[sl, :]
                t_ref[b, sl, :] = score
                part = rows8(jnp.max, score)
                top = part if top is None else jnp.maximum(top, part)
            top = jnp.max(top, axis=0, keepdims=True)
            total = jnp.zeros((8, LOC), F32)
            mixed = jnp.zeros((8, LOC), F32)
            for sl in chunks:
                e = jnp.exp2(t_ref[b, sl, :] - top)
                t_ref[b, sl, :] = e
                total = total + rows8(jnp.sum, e)
                mixed = mixed + rows8(jnp.sum, e * dp_ref[b, sl, :])
            inv_total = 1.0 / jnp.sum(total, axis=0, keepdims=True)
            delta = jnp.sum(mixed, axis=0, keepdims=True) * inv_total
            for sl in chunks:
                p = t_ref[b, sl, :] * inv_total
                ds_ref[b, sl, :] = (p * (dp_ref[b, sl, :] - delta)).astype(BF16)
                p_ref[b, sl, :] = p.astype(BF16)

        def gradients(h, b):
            dk_acc[...] += dot_nn(ds_ref[b], rq_ref[b])
            dv_acc[...] += dot_nn(p_ref[b], og_v[:, head_columns(h)])
            dq = dot_nn(kt[...], ds_ref[b]).T * inv_root
            dq = dq * cos_ref[...] - pltpu.roll(dq, HD // 2, 1) * sin_ref[...]
            dq_v[:, head_columns(h)] = dq.astype(BF16)

        def two_heads(i, carry):
            for b in range(2):
                products(2 * i + b, b)
            for b in range(2):
                softmax(b)
            for b in range(2):
                gradients(2 * i + b, b)
            return carry

        lax.fori_loop(0, GROUP // 2, two_heads, 0)

        kg_own[g] = dk_acc[0:LOC, :] * inv_root
        dv_own[g] = dv_acc[0:LOC, :]
        for k in range(1, BACK + 1):
            rows = slice(k * LOC, (k + 1) * LOC)
            term_send[g, 0, k - 1] = (dk_acc[rows, :] * inv_root).astype(BF16)
            term_send[g, 1, k - 1] = dv_acc[rows, :].astype(BF16)
        for kind in range(2):
            for k in range(BACK, 0, -1):
                @pl.when(c >= k)
                def _(k=k, g=g, kind=kind):
                    term_copy(g, kind, k).start()

    dq_copy = pltpu.make_async_copy(dq_v, dq_hbm, local_sem.at[7])
    dq_copy.start()
    sent.append(dq_copy.wait)

    def kg_copy(k, g):
        part = kgt.at[z, pl.ds(g * HD, HD), :]
        return remote(part, part, kg_send_sem.at[k, g], kg_recv_sem.at[k, g], z_peer(k))

    for g in range(KVH):
        for k in range(1, BACK + 1):
            @pl.when(c + k < NCTX)
            def _(k=k, g=g):
                term_copy(g, 0, k).wait_recv()
                kg_own[g] = kg_own[g] + term_recv[g, 0, k - 1].astype(F32)
        kg = kg_own[g]
        kg = kg * cosv - pltpu.roll(kg, HD // 2, 1) * sinv
        kgt[z, pl.ds(g * HD, HD), :] = kg.T.astype(BF16)
        for k in (4, 3, 5, 2, 6, 1, 7):
            kg_copy(k, g).start()

    def xf_copy(k):
        rows = pl.ds(pl.multiple_of(lax.rem(z + NZ - k, NZ) * LOC, LOC), LOC)
        part = xr.at[t, :, rows, :]
        return remote(part, part, xf_send_sem.at[k], xf_recv_sem.at[k], (c, d, 1 - t))

    def x_forward(k):
        if k == 0:
            for copy in x_own:
                copy.wait()
        else:
            x_copy(k, 0).wait_recv()
            x_copy(k, 1).wait_recv()
        xf_copy(k).start()

    for g in range(KVH):
        for k in range(1, BACK + 1):
            @pl.when(c + k < NCTX)
            def _(k=k, g=g):
                term_copy(g, 1, k).wait_recv()
                dv_own[g] = dv_own[g] + term_recv[g, 1, k - 1].astype(F32)
        dv_out[:, g * HD:(g + 1) * HD] = dv_own[g].astype(BF16)

    sources = (0, 1, 7, 2, 6, 3, 5, 4)
    x_forward(sources[0])
    for g in range(KVH):
        sent.append(lambda g=g: over(1, NZ, lambda k: kg_copy(k, g).wait_send()))
    sent.append(lambda: over(0, NZ, lambda k: xf_copy(k).wait_send()))

    for n, k in enumerate(sources):
        if n + 1 < NZ:
            x_forward(sources[n + 1])
        for g in range(KVH):
            if k > 0:
                kg_copy(k, g).wait_recv()
        xf_copy(k).wait_recv()
        source = lax.rem(z + NZ - k, NZ)
        tokens = pl.ds(pl.multiple_of(source * LOC, LOC), LOC)
        for i in range(2):
            for h in range(2):
                rows = slice(h * LOC, (h + 1) * LOC)
                term = dot_nn(kgt[source], xr[h, i, tokens, :])
                if n > 0:
                    term = term + gacc[i, :, rows]
                if n + 1 < NZ:
                    gacc[i, :, rows] = term
                else:
                    gtb[i, :, rows] = term.astype(BF16)

    part_rows = LOC // NCTX

    def rs_copy(k):
        p, device = plane_peer(k)
        return remote(
            gtb.at[p // NCTX, pl.ds(pl.multiple_of(lax.rem(p, NCTX) * part_rows, part_rows), part_rows), :],
            rbuf.at[k], rs_send_sem.at[k], rs_recv_sem.at[k], device,
        )

    def rs_start(k, carry):
        rs_copy(k).start()
        return carry

    lax.fori_loop(1, NPLANE, rs_start, 0)

    def rs_sum(k, total):
        rs_copy(k).wait_recv()
        return total + rbuf[k].astype(F32)

    sent.append(lambda: over(1, NPLANE, lambda k: rs_copy(k).wait_send()))
    own_rows = pl.ds(pl.multiple_of(c * part_rows, part_rows), part_rows)
    total = lax.fori_loop(1, NPLANE, rs_sum, gtb[xl, own_rows, :].astype(F32))
    gall[own_rows, :] = (total * (1.0 / math.sqrt(NDP * NCTX * LOC))).astype(BF16)

    def ga_copy(k):
        return remote(gall.at[own_rows, :], gall.at[own_rows, :], ga_send_sem.at[k], ga_recv_sem.at[k], ctx_peer(k))

    def ga_start(k, carry):
        ga_copy(k).start()
        return carry

    def ga_wait(k, carry):
        ga_copy(k).wait_recv()
        return carry

    lax.fori_loop(1, NCTX, ga_start, 0)
    for copy in opt_copies:
        copy.wait()
    lax.fori_loop(1, NCTX, ga_wait, 0)

    sent.append(lambda: over(1, NCTX, lambda k: ga_copy(k).wait_send()))
    for h in range(2):
        grad = gall[:, h * LOC:(h + 1) * LOC].astype(F32).T
        grad_out[h] = grad
        nms = adam(grad, opt_v[0, h], opt_v[1, h], opt_v[2, h])[0]
        wb[h] = nms.astype(BF16).reshape(NCTX, part_rows, LOC)

    keeps = [
        pltpu.make_async_copy(wb.at[0], kw_hbm.at[0, d], local_sem.at[8]),
        pltpu.make_async_copy(wb.at[1, c], kw_hbm.at[1, d, c], local_sem.at[9]),
    ]
    for keep in keeps:
        keep.start()

    def zs_copy(k):
        return remote(
            wb.at[1, c], kw_hbm.at[1, d, c], zs_send_sem.at[k], zs_recv_sem.at[k], z_peer(k),
        )

    swap = remote(wb.at[0], kw_hbm.at[0, d], sw_send_sem, sw_recv_sem, (c, (1 - xl) * NZ + z, t))

    def ring_copy(s, way, same, src=None):
        step = 1 if way == 0 else NZ - 1
        zb = lax.rem(z + (NZ - s if way == 0 else s), NZ)
        block = (xl if same else 1 - xl) * NZ + zb
        return remote(
            kw_hbm.at[0, block] if src is None else src, kw_hbm.at[0, block],
            ring_send_sem.at[way, s, int(same)], ring_recv_sem.at[way, s, int(same)], z_peer(step),
        )

    over(1, NZ, lambda k: zs_copy(k).start())
    swap.start()
    ring_copy(0, 0, True, wb.at[0]).start()
    ring_copy(0, 1, True, wb.at[0]).start()
    swap.wait_recv()
    ring_copy(0, 0, False).start()
    ring_copy(0, 1, False).start()
    over(1, NZ, lambda k: zs_copy(k).wait_recv())
    for keep in keeps:
        keep.wait()

    y = c // 2
    x = 2 * lax.rem(c, 2) + xl

    def chip(xx, yy):
        xx, yy = lax.rem(xx, 4), lax.rem(yy, 4)
        return (2 * yy + xx // 2, lax.rem(xx, 2) * NZ + z, t)

    def piece(xx, yy, first):
        xx, yy = lax.rem(xx, 4), lax.rem(yy, 4)
        return kw_hbm.at[1, pl.ds(lax.rem(xx, 2) * NZ + first * (NZ // 2), NZ // 2), 2 * yy + xx // 2]

    def stage1(first, j):
        part = piece(x, y, first)
        device = chip(x + j, y) if first == 0 else chip(x, y + j)
        return remote(part, part, s1_send_sem.at[first, j], s1_recv_sem.at[first, j], device)

    def stage2(first, a, j):
        part = piece(x + 4 - a, y, first) if first == 0 else piece(x, y + 4 - a, first)
        device = chip(x, y + j) if first == 0 else chip(x + j, y)
        return remote(part, part, s2_send_sem.at[first, a, j], s2_recv_sem.at[first, a, j], device)

    ring = [(s, way, same) for s in range(4) for same in (True, False) for way in range(2) if s < 3 or same == (way == 0)]

    def ring_step(step):
        for s, way, same in ring:
            if s == step:
                ring_copy(s, way, same).wait_recv()
                if (s + 1, way, same) in ring:
                    ring_copy(s + 1, way, same).start()

    for j in (2, 1, 3):
        for first in range(2):
            stage1(first, j).start()
    for j in (2, 1, 3):
        for first in range(2):
            stage2(first, 0, j).start()
    ring_step(0)
    for step, a in enumerate((1, 3, 2)):
        for first in range(2):
            stage1(first, a).wait_recv()
            over(1, 4, lambda j: stage2(first, a, j).start())
        ring_step(step + 1)
    for first in range(2):
        for a in range(4):
            over(1, 4, lambda j: stage2(first, a, j).wait_recv())

    sent.append(swap.wait_send)
    sent.append(lambda: over(1, NZ, lambda k: zs_copy(k).wait_send()))
    sent.extend(ring_copy(s, way, same).wait_send for s, way, same in ring)
    for first in range(2):
        sent.append(lambda first=first: over(1, 4, lambda j: stage1(first, j).wait_send()))
        for a in range(4):
            sent.append(lambda first=first, a=a: over(1, 4, lambda j: stage2(first, a, j).wait_send()))

    for wait in sent:
        wait()


def on_device(
    layer_input, queries, keys, values, out_grad, doc_ids, freq_bins, master, moment1, moment2
):
    positions = lax.axis_index("ctx") * LOC + jnp.arange(LOC, dtype=jnp.int32)
    angles = positions.astype(F32)[:, None] * frequencies(freq_bins)[None, :]
    cosine = jnp.cos(angles) * magnitude_scale
    sine = jnp.sin(angles) * magnitude_scale
    cosine = jnp.concatenate([cosine, cosine], axis=1)
    sine = jnp.concatenate([-sine, sine], axis=1)

    any_ = pl.BlockSpec(memory_space=pl.ANY)
    vmem = pl.BlockSpec(memory_space=pltpu.VMEM)
    dma = pltpu.SemaphoreType.DMA
    part_rows = LOC // NCTX
    rows, cols = 2, LOC
    dq, dv, grad, kw = pl.pallas_call(
        kernel,
        out_shape=(
            jax.ShapeDtypeStruct((LOC, KVH * GROUP * HD), BF16),
            jax.ShapeDtypeStruct((LOC, KVH * HD), BF16),
            jax.ShapeDtypeStruct((rows, LOC, cols), F32),
            jax.ShapeDtypeStruct((2, NDP, NCTX, part_rows, cols), BF16),
        ),
        in_specs=[any_, any_, vmem, vmem, vmem, vmem, vmem, any_, any_, any_, any_],
        out_specs=(any_, vmem, vmem, any_),
        scratch_shapes=[
            pltpu.VMEM((LOC, KVH * GROUP * HD), BF16),
            pltpu.VMEM((LOC, KVH * GROUP * HD), BF16),
            pltpu.VMEM((LOC, KVH * GROUP * HD), BF16),
            pltpu.VMEM((KVH, 2, WIN, HD), BF16),
            pltpu.VMEM((HD, WIN), BF16),
            pltpu.VMEM((BACK + 1, 8, LOC), jnp.int32),
            pltpu.VMEM((WIN, LOC), F32),
            pltpu.VMEM((2, LOC, HD), BF16),
            pltpu.VMEM((2, WIN, LOC), F32),
            pltpu.VMEM((2, WIN, LOC), F32),
            pltpu.VMEM((2, WIN, LOC), BF16),
            pltpu.VMEM((2, WIN, LOC), BF16),
            pltpu.VMEM((WIN, HD), F32),
            pltpu.VMEM((WIN, HD), F32),
            pltpu.VMEM((KVH, 2, BACK, LOC, HD), BF16),
            pltpu.VMEM((KVH, 2, BACK, LOC, HD), BF16),
            pltpu.VMEM((KVH, LOC, HD), F32),
            pltpu.VMEM((KVH, LOC, HD), F32),
            pltpu.VMEM((2, 2, NZ * LOC, LOC), BF16),
            pltpu.VMEM((NZ, LOC, LOC), BF16),
            pltpu.VMEM((2, LOC, 2 * LOC), F32),
            pltpu.VMEM((2, LOC, 2 * LOC), BF16),
            pltpu.VMEM((NPLANE, part_rows, 2 * LOC), BF16),
            pltpu.VMEM((LOC, 2 * LOC), BF16),
            pltpu.VMEM((3, 2, LOC, LOC), F32),
            pltpu.VMEM((2, NCTX, part_rows, LOC), BF16),
            dma((10,)),
            dma((BACK,)), dma((BACK,)),
            dma((KVH, BACK)), dma((KVH, BACK)),
            dma((NZ, 2)), dma((NZ, 2)),
            dma((NZ,)), dma((NZ,)),
            dma((KVH, 2, BACK)), dma((KVH, 2, BACK)),
            dma((NZ, KVH)), dma((NZ, KVH)),
            dma((NPLANE,)), dma((NPLANE,)),
            dma((NCTX,)), dma((NCTX,)),
            dma, dma,
            dma((2, 4, 2)), dma((2, 4, 2)),
            dma((NZ,)), dma((NZ,)),
            dma((2, 4)), dma((2, 4)),
            dma((2, 4, 4)), dma((2, 4, 4)),
        ],
        compiler_params=pltpu.CompilerParams(
            collective_id=0, has_side_effects=True, vmem_limit_bytes=54 * 1024 * 1024
        ),
    )(
        queries[0], out_grad[0], keys[0], values[0], doc_ids, cosine, sine, layer_input[0],
        master, moment1, moment2,
    )
    new_master, new_moment1, new_moment2 = adam(grad, master, moment1, moment2)
    return (dq[None], dv[None], new_master, new_moment1, new_moment2, kw.reshape(2, NDP * LOC, cols))


def solution(mesh):
    placed = (
        P("dp", "ctx", "tp"),
        P("dp", "ctx", "tp"),
        P("dp", "ctx", "tp"),
        P("dp", "ctx", "tp"),
        P("dp", "ctx", "tp"),
        P("dp", "ctx"),
        P(),
        P(None, "dp", "tp"),
        P(None, "dp", "tp"),
        P(None, "dp", "tp"),
    )
    return jax.shard_map(
        on_device,
        mesh=mesh,
        in_specs=placed,
        out_specs=(
            P("dp", "ctx", "tp"),
            P("dp", "ctx", "tp"),
            P(None, "dp", "tp"),
            P(None, "dp", "tp"),
            P(None, "dp", "tp"),
            P(None, None, "tp"),
        ),
        check_vma=False,
    )
```
